32 devices in a mesh: leaf: 8 (over z, core), bond: 4 (over y, x).
Axes of the slice: x: 2, y: 2, z: 4, core: 2. Of those that a mesh axis runs over, the one named last changes fastest.
Arguments:
- isometries: bfloat16 [8, 256, 256, 256], P('leaf', 'bond'), may hold values from -0.1875 to 0.1875
- leaf_ops: bfloat16 [8, 1, 256, 256], P('leaf', None, 'bond'), may hold values from -6 to 6
- charges: int32 [8, 3, 4], P('leaf'), may hold values from 0 to 3
- assign: int32 [8, 1], P('leaf'), may hold values from 0 to 2
Outputs:
- node_ops: bfloat16 [8, 1, 256, 256], P('leaf', None, 'bond')
The draws below stay inside these ranges and needn't reach their ends.
Inputs may be any that keep to these rules, and one draw needn't show every extreme that they name: `assign`: 0 takes the left child's operator, 1 the right child's, 2 their sum.
All inputs are finite; a program needn't handle non-finite values.
Results may differ from the reference program's by a relative error of at most 0.008.
Values may be sent and summed in bfloat16 or wider, within the bound.
No kernel may reach another device: no remote copies, remote signals or barrier semaphores. Data moves between devices by JAX's collectives and lax.ppermute only.
A program may use at most 128 MiB of HBM per device.

```python
import jax
import jax.numpy as jnp
from jax import lax

CHI = 256
BLOCK = 64
QMOD = 4
OPS = 1
LEVELS = 3
NBLK = 4
SLOTS = 8


def touch_ends(values, stream_key, least, largest):
    spot = [jax.random.randint(jax.random.fold_in(stream_key, axis), (), 0, length) for axis, length in enumerate(values.shape)]
    main_axis = values.shape.index(max(values.shape))
    beside = spot[:main_axis] + [(spot[main_axis] + 1) % values.shape[main_axis]] + spot[main_axis + 1:]
    return values.at[tuple(spot)].set(least).at[tuple(beside)].set(largest)


def levels(key, dims, split, least, largest):
    gain = 1.0
    for axis_at, shards_of in split:
        draws = jax.random.uniform(jax.random.fold_in(jax.random.fold_in(key, 6), axis_at), (shards_of,), jnp.float32, least / len(split), largest / len(split))
        gain = gain * jnp.repeat(jnp.exp(draws), dims[axis_at] // shards_of).reshape((-1,) + (1,) * (len(dims) - 1 - axis_at))
    return gain


def gaussian(rng, dims, scale, reach, pieces=(), kind=jnp.bfloat16):
    gain = levels(rng, dims, pieces, -0.22, 0.18) if pieces else 1.0
    values = jax.random.normal(rng, dims, jnp.float32) * scale * gain
    return jnp.minimum(jnp.maximum(values, -reach), reach).astype(kind)


def setup_inputs(seed: int = 0) -> dict:
    splits = jax.random.split(jax.random.key(seed), 5)
    return {
        "isometries": gaussian(splits[0], (SLOTS, CHI, CHI, CHI), (4 * CHI) ** -0.5, 0.1875, ((0, 8), (1, 4))),
        "leaf_ops": gaussian(splits[1], (SLOTS, OPS, CHI, CHI), 1.0, 6.0, ((0, 8), (2, 4))),
        "charges": touch_ends(jax.random.randint(splits[2], (SLOTS, 3, NBLK), 0, QMOD), jax.random.fold_in(splits[2], 1), 0, QMOD - 1).astype(jnp.int32),
        "assign": touch_ends(jax.random.randint(splits[3], (SLOTS, OPS), 0, 3), jax.random.fold_in(splits[3], 1), 0, 2).astype(jnp.int32),
    }


def block_mask(charge_row):
    spread = jnp.repeat(charge_row, BLOCK, axis=1)
    charge_sum = spread[0][:, None, None] + spread[1][None, :, None] - spread[2][None, None, :]
    return jnp.mod(charge_sum, QMOD) == 0


def renormalize(weight, left_ops, right_ops, take_left, take_right):
    weight_wide = weight.astype(jnp.float32)
    left_mixed = jnp.einsum('kca,abq->kcbq', left_ops.astype(jnp.float32), weight_wide).astype(jnp.bfloat16)
    left_part = jnp.einsum('cbp,kcbq->kpq', weight_wide, left_mixed.astype(jnp.float32))
    right_mixed = jnp.einsum('kcb,abq->kacq', right_ops.astype(jnp.float32), weight_wide).astype(jnp.bfloat16)
    right_part = jnp.einsum('acp,kacq->kpq', weight_wide, right_mixed.astype(jnp.float32))
    combined = take_left[:, None, None] * left_part + take_right[:, None, None] * right_part
    return combined.astype(jnp.bfloat16)


def one_slot(packed):
    weight_raw, charge_row, assign_row, left_ops, right_ops = packed
    weight = jnp.where(block_mask(charge_row), weight_raw, jnp.zeros((), weight_raw.dtype))
    take_left = (assign_row != 1).astype(jnp.float32)
    take_right = (assign_row != 0).astype(jnp.float32)
    return renormalize(weight, left_ops, right_ops, take_left, take_right)


def reference(isometries, leaf_ops, charges, assign):
    held = leaf_ops.astype(jnp.bfloat16)
    for level_now in range(1, LEVELS + 1):
        reach_by = 2 ** (level_now - 1)
        left_all = jnp.roll(held, reach_by, axis=0)
        held = lax.map(one_slot, (isometries, charges, assign, left_all, held))
    return held
```

```python
import functools

import jax
import jax.numpy as jnp
from jax import lax
from jax.experimental import pallas as pl
from jax.experimental.pallas import tpu as pltpu
from jax.sharding import PartitionSpec as P

BLOCK = 64
QMOD = 4
LEVELS = 3
ROWS = 16
GROUP = 16
CHUNKS = 4
CAPACITIES = (4, 6, 8, 10, 12, 16)
F32 = jnp.float32
BF16 = jnp.bfloat16
MIB = 2**20
ANY = pl.BlockSpec(memory_space=pl.ANY)
VMEM = pl.BlockSpec(memory_space=pltpu.VMEM)
SMEM = pl.BlockSpec(memory_space=pltpu.SMEM)


def dot(a, b, ca, cb):
    return lax.dot_general(a, b, (((ca,), (cb,)), ((), ())), preferred_element_type=F32)


def passed_along(array, axis, by):
    devices = lax.axis_size(axis)
    return lax.ppermute(array, axis, [(i, (i + by) % devices) for i in range(devices)])


def swapped(array, mask):
    devices = lax.axis_size("bond")
    return lax.ppermute(array, "bond", [(i, i ^ mask) for i in range(devices)])


def lookup(index_vector, charge_table, blocks):
    hits = index_vector[:, None] == blocks[None, :]
    return jnp.sum(jnp.where(hits, charge_table[None, :], 0), axis=1)


def shards_plain(isometries, leaf_ops, charges, assign):
    bond_rank = lax.axis_index("bond")
    weight = isometries[0]
    slab_rows = weight.shape[0]
    bond_width = weight.shape[1]
    op_count = leaf_ops.shape[1]
    charge_row = charges[0]
    blocks = jnp.arange(charge_row.shape[1], dtype=jnp.int32)
    left_index = (bond_rank * slab_rows + jnp.arange(slab_rows, dtype=jnp.int32)) // BLOCK
    full_index = jnp.arange(bond_width, dtype=jnp.int32) // BLOCK
    charge_left = lookup(left_index, charge_row[0], blocks)
    charge_right = lookup(full_index, charge_row[1], blocks)
    charge_parent = lookup(full_index, charge_row[2], blocks)
    charge_sum = (
        charge_left[:, None, None] + charge_right[None, :, None] - charge_parent[None, None, :]
    )
    keep_mask = jnp.mod(charge_sum, QMOD) == 0
    masked = jnp.where(keep_mask, weight, jnp.zeros((), weight.dtype))
    by_right = lax.all_to_all(masked, "bond", split_axis=1, concat_axis=0, tiled=True)
    take_left = (assign[0] != 1).astype(F32)
    take_right = (assign[0] != 0).astype(F32)
    held_ops = lax.all_gather(leaf_ops[0], "bond", axis=1, tiled=True)
    for level_now in range(1, LEVELS + 1):
        reach_by = 2 ** (level_now - 1)
        left_ops = passed_along(held_ops, "leaf", reach_by)
        left_mixed = jnp.dot(
            left_ops.reshape(op_count * bond_width, bond_width),
            by_right.reshape(bond_width, -1),
            preferred_element_type=F32,
        ).astype(BF16)
        left_mixed = left_mixed.reshape(op_count, -1, bond_width)
        left_part = jnp.einsum(
            "rp,krq->kpq",
            by_right.reshape(-1, bond_width),
            left_mixed,
            preferred_element_type=F32,
        )
        right_mixed = jnp.einsum(
            "kcb,abq->kacq", held_ops, masked, preferred_element_type=F32
        ).astype(BF16)
        right_part = jnp.einsum("acp,kacq->kpq", masked, right_mixed, preferred_element_type=F32)
        partial_sum = take_left[:, None, None] * left_part + take_right[:, None, None] * right_part
        held_ops = lax.psum(partial_sum, "bond").astype(BF16)
    result = lax.dynamic_slice_in_dim(held_ops, bond_rank * slab_rows, slab_rows, 1)
    return result[None]


def add_group(op, mats, total):
    count, width = mats.shape[0], mats.shape[1]
    mixed = [dot(op, mats[j], 1, 0).astype(BF16) for j in range(count)]
    return total + dot(
        mats.reshape(count * width, width), jnp.concatenate(mixed, 0), 0, 0
    )


def pack_kernel(cap, chunks, info, table, weight, *rest):
    outs, select, turn = rest[:-2], rest[-2], rest[-1]
    rank = info[0]
    width = weight.shape[-1]
    blocks = weight.shape[1]
    area = GROUP * ROWS

    @pl.when(pl.program_id(0) == 0)
    def _():
        target = table[rank]
        for k in range(blocks):
            row = lax.broadcasted_iota(jnp.int32, (width, cap * BLOCK), 0) + k * width
            select[k * width : (k + 1) * width, :] = jnp.where(row == target, 1.0, 0.0).astype(BF16)
        to = lax.broadcasted_iota(jnp.int32, (area, area), 0)
        at = lax.broadcasted_iota(jnp.int32, (area, area), 1)
        moved = (to % GROUP) * ROWS + to // GROUP
        turn[...] = jnp.where(at == moved, 1.0, 0.0).astype(BF16)

    partners = weight.shape[2]
    each = ROWS // chunks
    for m in range(partners):
        to = rank ^ m
        wide = jnp.concatenate(
            [weight[:, k, to].reshape(area, width) for k in range(blocks)], axis=1
        )
        taken = dot(wide, select[...], 1, 0).astype(BF16)
        turned = dot(turn[...], taken, 1, 0).astype(BF16)
        for c in range(chunks):
            part = turned[c * each * GROUP : (c + 1) * each * GROUP]
            outs[m * chunks + c][...] = part.reshape(each, GROUP, cap * BLOCK)


def pack(cap, rank, table, weight):
    slab, width = weight.shape[0], weight.shape[1]
    partners = lax.axis_size("bond")
    blocks = width // BLOCK
    cut = weight.reshape(slab, blocks, partners, ROWS, width)
    each = ROWS // CHUNKS
    lanes = cap * BLOCK
    return pl.pallas_call(
        functools.partial(pack_kernel, cap, CHUNKS),
        grid=(slab // GROUP,),
        in_specs=[
            SMEM,
            pl.BlockSpec((partners, 1, lanes), lambda i: (0, 0, 0)),
            pl.BlockSpec((GROUP, blocks, partners, ROWS, width), lambda i: (i, 0, 0, 0, 0)),
        ],
        out_specs=[pl.BlockSpec((each, GROUP, lanes), lambda i: (0, i, 0))] * (partners * CHUNKS),
        out_shape=[jax.ShapeDtypeStruct((each, slab, lanes), BF16)] * (partners * CHUNKS),
        scratch_shapes=[
            pltpu.VMEM((width * blocks, lanes), BF16),
            pltpu.VMEM((GROUP * ROWS, GROUP * ROWS), BF16),
        ],
        compiler_params=pltpu.CompilerParams(vmem_limit_bytes=40 * MIB),
        name="pack",
    )(rank.reshape(1), table, cut)


def first_left_kernel(cap, info, table, op, before, *rest):
    partners = table.shape[0]
    parts, mats, after = rest[:partners], rest[partners], rest[partners + 1]
    each, slab, lanes = parts[0].shape
    width = op.shape[0]
    blocks = width // BLOCK
    rank = info[0]
    for m in range(partners):
        source = rank ^ m
        target = table[source]
        rows = parts[m][...].reshape(each * slab, lanes)
        for k in range(blocks):
            row = lax.broadcasted_iota(jnp.int32, (width, lanes), 0) + k * width
            select = jnp.where(row == target, 1.0, 0.0).astype(BF16)
            placed = dot(rows, select, 1, 1).astype(BF16).reshape(each, slab, width)
            mats[k * each : (k + 1) * each, pl.ds(pl.multiple_of(source * slab, slab), slab), :] = placed
    after[...] = add_group(op[...], mats[...], before[...])


def first_left(cap, rank, table, op, before, parts):
    partners = len(parts)
    each, slab, lanes = parts[0].shape
    width = op.shape[0]
    count = each * (width // BLOCK)
    return pl.pallas_call(
        functools.partial(first_left_kernel, cap),
        in_specs=[SMEM, VMEM, VMEM, VMEM] + [VMEM] * partners,
        out_specs=[VMEM, VMEM],
        out_shape=[
            jax.ShapeDtypeStruct((count, width, width), BF16),
            jax.ShapeDtypeStruct((width, width), F32),
        ],
        compiler_params=pltpu.CompilerParams(vmem_limit_bytes=40 * MIB),
        name="first_left",
    )(rank.reshape(1), table, op, before, *parts)


def side_kernel(masked, pieces, per, info, op, before, *rest):
    mask = rest[0] if masked else None
    mats = rest[masked : masked + pieces]
    after, held, sems = rest[masked + pieces :]
    loads = held.shape[0]

    def load(c):
        if pieces == 1:
            source = mats[0].at[pl.ds(c * per, per)]
        else:
            source = mats[c]
        return pltpu.make_async_copy(source, held.at[c], sems.at[c])

    after[...] = before[...]

    @pl.when(info[0] != 0)
    def _():
        for c in range(loads):
            load(c).start()
        for c in range(loads):
            load(c).wait()
            group = held[c]
            if masked:
                group = group * mask[...][None]
            after[...] = add_group(op[...], group, after[...])


def side(flag, op, before, mats, mask=None):
    width = op.shape[0]
    total = sum(m.shape[0] for m in mats)
    per = mats[0].shape[0] if len(mats) > 1 else min(GROUP, total)
    masked = mask is not None
    return pl.pallas_call(
        functools.partial(side_kernel, int(masked), len(mats), per),
        in_specs=[SMEM, VMEM, VMEM] + [VMEM] * masked + [ANY] * len(mats),
        out_specs=VMEM,
        out_shape=jax.ShapeDtypeStruct((width, width), F32),
        scratch_shapes=[
            pltpu.VMEM((total // per, per, width, width), BF16),
            pltpu.SemaphoreType.DMA((total // per,)),
        ],
        compiler_params=pltpu.CompilerParams(vmem_limit_bytes=30 * MIB),
        cost_estimate=pl.CostEstimate(
            flops=4 * total * width**3, bytes_accessed=2 * total * width**2, transcendentals=0
        ),
        name="side",
    )(flag.reshape(1), op, before, *([mask] if masked else []), *mats)


def shards(isometries, leaf_ops, charges, assign):
    rank = lax.axis_index("bond")
    partners = lax.axis_size("bond")
    weight = isometries[0]
    slab, width = weight.shape[0], weight.shape[1]
    blocks = width // BLOCK
    row = charges[0]
    takes_left = (assign[0, 0] != 1).astype(jnp.int32)
    takes_right = (assign[0, 0] != 0).astype(jnp.int32)
    own = leaf_ops[0, 0]
    left = passed_along(own, "leaf", 1)

    allowed = (
        jnp.mod(row[0][:, None, None] + row[1][None, :, None] - row[2][None, None, :], QMOD) == 0
    )
    flat = allowed.reshape(blocks, blocks * blocks)
    place = jnp.cumsum(flat.astype(jnp.int32), axis=1) - 1
    need = jnp.max(place[:, -1]) + 1
    index = jnp.arange(blocks * blocks, dtype=jnp.int32)
    slots = jnp.arange(blocks * blocks, dtype=jnp.int32)
    hit = flat[:, None, :] & (place[:, None, :] == slots[None, :, None])
    base = jnp.sum(jnp.where(hit, index[None, None, :] + 1, 0), axis=2) - 1
    spread = jnp.where(
        base[:, :, None] >= 0,
        base[:, :, None] * BLOCK + jnp.arange(BLOCK, dtype=jnp.int32)[None, None, :],
        -1,
    ).reshape(blocks, 1, blocks * blocks * BLOCK)
    mine = lax.dynamic_index_in_dim(allowed, rank, 0, keepdims=False).astype(BF16)
    mask = jnp.repeat(jnp.repeat(mine, BLOCK, axis=0), BLOCK, axis=1)
    zeros = jnp.zeros((width, width), F32)

    def gathered(part):
        both = [part] + [swapped(part, m) for m in range(1, partners)]
        both = jnp.stack(both)
        order = jnp.arange(partners) ^ rank
        return jnp.take(both, order, axis=0)

    def ops_of(own, left):
        full = gathered(jnp.stack([own, left]))
        return full[:, 0].reshape(width, width), full[:, 1].reshape(width, width)

    def without(weight, own, left, mask, spread):
        op, _ = ops_of(own, left)
        total = side(takes_right, op, zeros, [weight], mask)
        count = slab // CHUNKS
        return total, *[jnp.zeros((count, width, width), BF16) for _ in range(CHUNKS)]

    def with_left(cap, weight, own, left, mask, spread):
        op, left_op = ops_of(own, left)
        table = spread[:, :, : cap * BLOCK]
        packed = pack(cap, rank, table, weight)
        chunks = []
        for c in range(CHUNKS):
            mine = [packed[m * CHUNKS + c] for m in range(partners)]
            chunks.append([mine[0]] + [swapped(mine[m], m) for m in range(1, partners)])
        total = side(takes_right, op, zeros, [weight], mask)
        mats = []
        for c in range(CHUNKS):
            mat, total = first_left(cap, rank, table, left_op, total, chunks[c])
            mats.append(mat)
        return total, *mats

    steps = sum((need > c).astype(jnp.int32) for c in CAPACITIES[:-1])
    branch = jnp.where(takes_left == 0, 0, steps + 1)
    total, *mats = lax.switch(
        branch,
        [without] + [functools.partial(with_left, c) for c in CAPACITIES],
        weight, own, left, mask, spread,
    )
    for level in range(2, LEVELS + 1):
        sent = total.astype(BF16)
        come = [swapped(sent, m) for m in range(1, partners)]
        op = (total + sum(c.astype(F32) for c in come)).astype(BF16)
        left_op = passed_along(op, "leaf", 2 ** (level - 1))
        total = side(takes_right, op, zeros, [weight], mask)
        total = side(takes_left, left_op, total, mats)

    def rows_of(m):
        return lax.dynamic_slice_in_dim(total, (rank ^ m) * slab, slab, 0)

    result = rows_of(0)
    for m in range(1, partners):
        result = result + swapped(rows_of(m), m)
    return result.astype(BF16)[None, None]


def solution(mesh):
    in_specs = (
        P("leaf", "bond", None, None),
        P("leaf", None, "bond", None),
        P("leaf", None, None),
        P("leaf", None),
    )
    out_specs = P("leaf", None, "bond", None)
    partners = mesh.shape["bond"]

    def whole(isometries, leaf_ops, charges, assign):
        width = isometries.shape[1]
        fits = (
            partners & (partners - 1) == 0
            and width // partners == BLOCK
            and BLOCK == partners * ROWS
            and charges.shape[2] * BLOCK == width
            and leaf_ops.shape[1] == 1
        )
        return jax.shard_map(
            shards if fits else shards_plain,
            mesh=mesh, in_specs=in_specs, out_specs=out_specs, check_vma=False,
        )(isometries, leaf_ops, charges, assign)

    return whole
```

```python
import functools

import jax
import jax.numpy as jnp
from jax import lax
from jax.experimental import pallas as pl
from jax.experimental.pallas import tpu as pltpu
from jax.sharding import PartitionSpec as P

BLOCK = 64
QMOD = 4
LEVELS = 3
ROWS = 16
GROUP = 16
CAPACITIES = (4, 6, 8, 10, 12, 16)
F32 = jnp.float32
BF16 = jnp.bfloat16
MIB = 2**20
ANY = pl.BlockSpec(memory_space=pl.ANY)
VMEM = pl.BlockSpec(memory_space=pltpu.VMEM)
SMEM = pl.BlockSpec(memory_space=pltpu.SMEM)


def dot(a, b, ca, cb):
    return lax.dot_general(a, b, (((ca,), (cb,)), ((), ())), preferred_element_type=F32)


def passed_along(array, axis, by):
    devices = lax.axis_size(axis)
    return lax.ppermute(array, axis, [(i, (i + by) % devices) for i in range(devices)])


def swapped(array, mask):
    devices = lax.axis_size("bond")
    return lax.ppermute(array, "bond", [(i, i ^ mask) for i in range(devices)])


def lookup(index_vector, charge_table, blocks):
    hits = index_vector[:, None] == blocks[None, :]
    return jnp.sum(jnp.where(hits, charge_table[None, :], 0), axis=1)


def shards_plain(isometries, leaf_ops, charges, assign):
    bond_rank = lax.axis_index("bond")
    weight = isometries[0]
    slab_rows = weight.shape[0]
    bond_width = weight.shape[1]
    op_count = leaf_ops.shape[1]
    charge_row = charges[0]
    blocks = jnp.arange(charge_row.shape[1], dtype=jnp.int32)
    left_index = (bond_rank * slab_rows + jnp.arange(slab_rows, dtype=jnp.int32)) // BLOCK
    full_index = jnp.arange(bond_width, dtype=jnp.int32) // BLOCK
    charge_left = lookup(left_index, charge_row[0], blocks)
    charge_right = lookup(full_index, charge_row[1], blocks)
    charge_parent = lookup(full_index, charge_row[2], blocks)
    charge_sum = (
        charge_left[:, None, None] + charge_right[None, :, None] - charge_parent[None, None, :]
    )
    keep_mask = jnp.mod(charge_sum, QMOD) == 0
    masked = jnp.where(keep_mask, weight, jnp.zeros((), weight.dtype))
    by_right = lax.all_to_all(masked, "bond", split_axis=1, concat_axis=0, tiled=True)
    take_left = (assign[0] != 1).astype(F32)
    take_right = (assign[0] != 0).astype(F32)
    held_ops = lax.all_gather(leaf_ops[0], "bond", axis=1, tiled=True)
    for level_now in range(1, LEVELS + 1):
        reach_by = 2 ** (level_now - 1)
        left_ops = passed_along(held_ops, "leaf", reach_by)
        left_mixed = jnp.dot(
            left_ops.reshape(op_count * bond_width, bond_width),
            by_right.reshape(bond_width, -1),
            preferred_element_type=F32,
        ).astype(BF16)
        left_mixed = left_mixed.reshape(op_count, -1, bond_width)
        left_part = jnp.einsum(
            "rp,krq->kpq",
            by_right.reshape(-1, bond_width),
            left_mixed,
            preferred_element_type=F32,
        )
        right_mixed = jnp.einsum(
            "kcb,abq->kacq", held_ops, masked, preferred_element_type=F32
        ).astype(BF16)
        right_part = jnp.einsum("acp,kacq->kpq", masked, right_mixed, preferred_element_type=F32)
        partial_sum = take_left[:, None, None] * left_part + take_right[:, None, None] * right_part
        held_ops = lax.psum(partial_sum, "bond").astype(BF16)
    result = lax.dynamic_slice_in_dim(held_ops, bond_rank * slab_rows, slab_rows, 1)
    return result[None]


CHARGES_AT = 2


def fits(info, blocks, left, right, parent):
    total = (
        info[CHARGES_AT + left]
        + info[CHARGES_AT + blocks + right]
        - info[CHARGES_AT + 2 * blocks + parent]
    )
    return lax.rem(total + QMOD, QMOD) == 0


def pieces_before(info, blocks, left, right, parent):
    count = jnp.int32(0)
    for k in range(blocks):
        for p in range(blocks):
            ahead = (k * blocks + p) < (right * blocks + parent)
            count += (fits(info, blocks, left, k, p) & ahead).astype(jnp.int32)
    return count


def pieces_of(info, blocks, left):
    return pieces_before(info, blocks, left, blocks, 0)


def add_group(op, mats, total):
    count, width = mats.shape[0], mats.shape[1]
    mixed = [dot(op, mats[j], 1, 0).astype(BF16) for j in range(count)]
    return total + dot(
        mats.reshape(count * width, width), jnp.concatenate(mixed, 0), 0, 0
    )


def halves_swapped(x):
    return jnp.concatenate([x[..., BLOCK:], x[..., :BLOCK]], axis=-1)


def pack_kernel(blocks, partners, info, weight, branch, *rest):
    groups = len(CAPACITIES)
    outs = rest[: partners * groups]
    stage, turn, sems = rest[partners * groups :]
    m, k = pl.program_id(0), pl.program_id(1)
    rank = info[0]
    area = GROUP * ROWS
    slab = weight.shape[0]
    width = weight.shape[-1]

    @pl.when((m == 0) & (k == 0))
    def _():
        to = lax.broadcasted_iota(jnp.int32, (area, area), 0)
        at = lax.broadcasted_iota(jnp.int32, (area, area), 1)
        turn[...] = jnp.where(at == (to % GROUP) * ROWS + to // GROUP, 1.0, 0.0).astype(BF16)
        need = lax.fori_loop(
            0, blocks, lambda d, most: jnp.maximum(most, pieces_of(info, blocks, d)), jnp.int32(0)
        )
        step = jnp.int32(1)
        for cap in CAPACITIES[:-1]:
            step += (need > cap).astype(jnp.int32)
        branch[0] = jnp.where(info[1] == 1, 0, step)

    allowed = [fits(info, blocks, rank, k, p) for p in range(blocks)]
    some = functools.reduce(jnp.logical_or, allowed)

    @pl.when(some & (info[1] != 1))
    def _():
        turned = []
        for g in range(slab // GROUP):
            rows = weight[g * GROUP : (g + 1) * GROUP].reshape(area, width)
            turned.append(dot(turn[...], rows, 1, 0).astype(BF16))
        half = len(turned) // 2
        slot = pieces_before(info, blocks, rank, k, 0)
        for p in range(blocks):

            @pl.when(allowed[p])
            def _():
                for h in range(half):
                    low = turned[h][:, p * BLOCK : (p + 1) * BLOCK]
                    high = turned[h + half][:, p * BLOCK : (p + 1) * BLOCK]
                    both = jnp.concatenate([low, high], axis=1).reshape(ROWS, GROUP, 2 * BLOCK)
                    stage[m, k * blocks + p, :, h * GROUP : (h + 1) * GROUP, :] = both
                first = 0
                for g, cap in enumerate(CAPACITIES):
                    for n in range(partners):

                        @pl.when((slot >= first) & (slot < cap) & (m == n))
                        def _():
                            pltpu.make_async_copy(
                                stage.at[n, k * blocks + p],
                                outs[n * groups + g].at[slot - first],
                                sems.at[n, k * blocks + p],
                            ).start()

                    first = cap

            slot = slot + allowed[p].astype(jnp.int32)

    @pl.when((m == partners - 1) & (k == blocks - 1) & (info[1] != 1))
    def _():
        @pl.loop(0, blocks * blocks)
        def _(f):
            @pl.when(fits(info, blocks, rank, f // blocks, f % blocks))
            def _():
                for n in range(partners):
                    pltpu.make_async_copy(
                        stage.at[n, f], outs[n * groups].at[0], sems.at[n, f]
                    ).wait()


def pack(info, weight):
    slab, width = weight.shape[0], weight.shape[1]
    partners = lax.axis_size("bond")
    blocks = width // BLOCK
    cut = weight.reshape(slab, blocks, partners, ROWS, width)
    sizes = [b - a for a, b in zip((0,) + CAPACITIES[:-1], CAPACITIES)]
    piece = (ROWS, slab // 2, 2 * BLOCK)
    branch, *packed = pl.pallas_call(
        functools.partial(pack_kernel, blocks, partners),
        grid_spec=pltpu.PrefetchScalarGridSpec(
            num_scalar_prefetch=1,
            grid=(partners, blocks),
            in_specs=[
                pl.BlockSpec(
                    (slab, None, None, ROWS, width), lambda m, k, info: (0, k, info[0] ^ m, 0, 0)
                )
            ],
            out_specs=[SMEM] + [ANY] * (partners * len(sizes)),
            scratch_shapes=[
                pltpu.VMEM((partners, blocks * blocks) + piece, BF16),
                pltpu.VMEM((GROUP * ROWS, GROUP * ROWS), BF16),
                pltpu.SemaphoreType.DMA((partners, blocks * blocks)),
            ],
        ),
        out_shape=[jax.ShapeDtypeStruct((1,), jnp.int32)]
        + [jax.ShapeDtypeStruct((n,) + piece, BF16) for n in sizes] * partners,
        compiler_params=pltpu.CompilerParams(vmem_limit_bytes=24 * MIB),
        name="pack",
    )(info, cut)
    groups = len(sizes)
    return branch[0], [packed[m * groups : (m + 1) * groups] for m in range(partners)]


def first_left_kernel(partners, info, op, before, *rest):
    groups = len(CAPACITIES)
    parts = rest[: partners * groups]
    mats, after, held, sems = rest[partners * groups :]
    rank = info[0]
    width = op.shape[0]
    blocks = width // BLOCK
    slab = 2 * held.shape[3]
    starts = (0,) + CAPACITIES[:-1]

    def load(m, g):
        return pltpu.make_async_copy(
            parts[m * groups + g],
            held.at[m, pl.ds(starts[g], CAPACITIES[g] - starts[g])],
            sems.at[m, g],
        )

    after[...] = before[...]

    @pl.when(info[1] != 1)
    def _():
        counts = [pieces_of(info, blocks, rank ^ m) for m in range(partners)]
        for m in range(partners):
            for g in range(groups):
                pl.when(counts[m] > starts[g])(load(m, g).start)

        @pl.loop(0, mats.shape[0])
        def _(j):
            mats[j] = jnp.zeros((width, width), BF16)

        for m in range(partners):
            for g in range(groups):
                pl.when(counts[m] > starts[g])(load(m, g).wait)

        @pl.loop(0, partners * blocks)
        def _(n):
            m, k = n // blocks, n % blocks
            source = rank ^ m
            slot = pieces_before(info, blocks, source, k, 0)
            for p in range(blocks):
                allowed = fits(info, blocks, source, k, p)

                @pl.when(allowed)
                def _():
                    piece = held[m, slot]
                    other = halves_swapped(piece)
                    tile = p // 2 * 2 * BLOCK
                    lane = lax.broadcasted_iota(jnp.int32, piece.shape, 2)
                    keep = lane < BLOCK if p % 2 == 0 else lane >= BLOCK
                    parts = (piece, other) if p % 2 == 0 else (other, piece)
                    for i, part in enumerate(parts):
                        at = pl.multiple_of(source * slab + i * (slab // 2), slab // 2)
                        where = (
                            pl.ds(pl.multiple_of(k * ROWS, ROWS), ROWS),
                            pl.ds(at, slab // 2),
                            slice(tile, tile + 2 * BLOCK),
                        )
                        mats[where] = jnp.where(keep, part, mats[where])

                slot = slot + allowed.astype(jnp.int32)

        @pl.loop(0, mats.shape[0] // GROUP)
        def _(c):
            group = mats[pl.ds(pl.multiple_of(c * GROUP, GROUP), GROUP)]
            after[...] = add_group(op[...], group, after[...])


def first_left(info, op, before, parts):
    partners, groups = len(parts), len(parts[0])
    width = op.shape[0]
    piece = parts[0][0].shape[1:]
    flat = [group for part in parts for group in part]
    return pl.pallas_call(
        functools.partial(first_left_kernel, partners),
        in_specs=[SMEM, VMEM, VMEM] + [ANY] * len(flat),
        out_specs=[VMEM, VMEM],
        out_shape=[
            jax.ShapeDtypeStruct((ROWS * (width // BLOCK), width, width), BF16),
            jax.ShapeDtypeStruct((width, width), F32),
        ],
        scratch_shapes=[
            pltpu.VMEM((partners, CAPACITIES[-1]) + piece, BF16),
            pltpu.SemaphoreType.DMA((partners, groups)),
        ],
        compiler_params=pltpu.CompilerParams(vmem_limit_bytes=32 * MIB),
        name="first_left",
    )(info, op, before, *flat)


def mask_of(info, width):
    blocks = width // BLOCK

    def spread(shape, axis, at):
        block = lax.broadcasted_iota(jnp.int32, shape, axis) // BLOCK
        charge = jnp.zeros(shape, jnp.int32)
        for k in range(blocks):
            charge = jnp.where(block == k, info[at + k], charge)
        return charge

    right = spread((width, width), 0, CHARGES_AT + blocks)
    parent = spread((width, width), 1, CHARGES_AT + 2 * blocks)
    left = info[CHARGES_AT + info[0]]
    return jnp.where(lax.rem(left + right - parent + QMOD, QMOD) == 0, 1.0, 0.0).astype(BF16)


def side_kernel(not_if, masked, per, info, op, before, mats, after, *scratch):
    after[...] = before[...]

    @pl.when(info[1] != not_if)
    def _():
        mask = mask_of(info, op.shape[0]) if masked else None
        if scratch:
            held, sems = scratch

            def load(c):
                return pltpu.make_async_copy(mats.at[pl.ds(c * per, per)], held.at[c], sems.at[c])

            @pl.loop(0, held.shape[0])
            def _(c):
                load(c).start()

        @pl.loop(0, mats.shape[0] // per)
        def _(c):
            if scratch:
                load(c).wait()
                group = held[c]
            else:
                group = mats[pl.ds(pl.multiple_of(c * per, per), per)]
            if masked:
                group = group * mask[None]
            after[...] = add_group(op[...], group, after[...])


def side(not_if, info, op, before, mats, masked, per, streamed):
    width = op.shape[0]
    total = mats.shape[0]
    return pl.pallas_call(
        functools.partial(side_kernel, not_if, masked, per),
        in_specs=[SMEM, VMEM, VMEM, ANY if streamed else VMEM],
        out_specs=VMEM,
        out_shape=jax.ShapeDtypeStruct((width, width), F32),
        scratch_shapes=[
            pltpu.VMEM((total // per, per, width, width), BF16),
            pltpu.SemaphoreType.DMA((total // per,)),
        ]
        if streamed
        else [],
        compiler_params=pltpu.CompilerParams(vmem_limit_bytes=(24 if streamed else 12) * MIB),
        cost_estimate=pl.CostEstimate(
            flops=4 * total * width**3, bytes_accessed=2 * total * width**2, transcendentals=0
        ),
        name="side",
    )(info, op, before, mats)


def shards(isometries, leaf_ops, charges, assign):
    rank = lax.axis_index("bond")
    partners = lax.axis_size("bond")
    weight = isometries[0]
    slab, width = weight.shape[0], weight.shape[1]
    own = leaf_ops[0, 0]
    left = passed_along(own, "leaf", 1)
    info = jnp.concatenate([rank.reshape(1).astype(jnp.int32), assign[0], charges[0].reshape(-1)])
    zeros = jnp.zeros((width, width), F32)

    def gathered(part):
        both = jnp.stack([part] + [swapped(part, m) for m in range(1, partners)])
        return jnp.take(both, jnp.arange(partners) ^ rank, axis=0)

    def ops_of(own, left):
        full = gathered(jnp.stack([own, left]))
        return full[:, 0].reshape(width, width), full[:, 1].reshape(width, width)

    branch, packed = pack(info, weight)

    def exchange(groups, info, weight, own, left, packed):
        op, left_op = ops_of(own, left)
        come = [
            [swapped(packed[m][g], m) for g in range(groups)]
            + [jnp.zeros_like(part) for part in packed[m][groups:]]
            for m in range(1, partners)
        ]
        total = side(0, info, op, zeros, weight, True, 8, True)
        return total, left_op, come

    total, left_op, come = lax.switch(
        branch,
        [functools.partial(exchange, g) for g in range(len(CAPACITIES) + 1)],
        info, weight, own, left, packed,
    )
    mats, total = first_left(info, left_op, total, [packed[0]] + come)
    for level in range(2, LEVELS + 1):
        sent = total.astype(BF16)
        come = [swapped(sent, m) for m in range(1, partners)]
        op = (total + sum(c.astype(F32) for c in come)).astype(BF16)
        left_op = passed_along(op, "leaf", 2 ** (level - 1))
        total = side(0, info, op, zeros, weight, True, 32, False)
        total = side(1, info, left_op, total, mats, False, 32, False)

    def rows_of(m):
        return lax.dynamic_slice_in_dim(total, (rank ^ m) * slab, slab, 0)

    result = rows_of(0)
    for m in range(1, partners):
        result = result + swapped(rows_of(m), m)
    return result.astype(BF16)[None, None]


def solution(mesh):
    in_specs = (
        P("leaf", "bond", None, None),
        P("leaf", None, "bond", None),
        P("leaf", None, None),
        P("leaf", None),
    )
    out_specs = P("leaf", None, "bond", None)
    partners = mesh.shape["bond"]

    def whole(isometries, leaf_ops, charges, assign):
        width = isometries.shape[1]
        fits = (
            partners & (partners - 1) == 0
            and width // partners == BLOCK
            and BLOCK == partners * ROWS
            and charges.shape[2] * BLOCK == width
            and leaf_ops.shape[1] == 1
        )
        return jax.shard_map(
            shards if fits else shards_plain,
            mesh=mesh, in_specs=in_specs, out_specs=out_specs, check_vma=False,
        )(isometries, leaf_ops, charges, assign)

    return whole
```

```python
import functools

import jax
import jax.numpy as jnp
from jax import lax
from jax.experimental import pallas as pl
from jax.experimental.pallas import tpu as pltpu
from jax.sharding import PartitionSpec as P

BLOCK = 64
QMOD = 4
LEVELS = 3
ROWS = 16
GROUP = 16
CAPACITIES = (4, 6, 8, 10, 12, 16)
F32 = jnp.float32
BF16 = jnp.bfloat16
MIB = 2**20
ANY = pl.BlockSpec(memory_space=pl.ANY)
VMEM = pl.BlockSpec(memory_space=pltpu.VMEM)
SMEM = pl.BlockSpec(memory_space=pltpu.SMEM)


def dot(a, b, ca, cb):
    return lax.dot_general(a, b, (((ca,), (cb,)), ((), ())), preferred_element_type=F32)


def passed_along(array, axis, by):
    devices = lax.axis_size(axis)
    return lax.ppermute(array, axis, [(i, (i + by) % devices) for i in range(devices)])


def swapped(array, mask):
    devices = lax.axis_size("bond")
    return lax.ppermute(array, "bond", [(i, i ^ mask) for i in range(devices)])


def lookup(index_vector, charge_table, blocks):
    hits = index_vector[:, None] == blocks[None, :]
    return jnp.sum(jnp.where(hits, charge_table[None, :], 0), axis=1)


def shards_plain(isometries, leaf_ops, charges, assign):
    bond_rank = lax.axis_index("bond")
    weight = isometries[0]
    slab_rows = weight.shape[0]
    bond_width = weight.shape[1]
    op_count = leaf_ops.shape[1]
    charge_row = charges[0]
    blocks = jnp.arange(charge_row.shape[1], dtype=jnp.int32)
    left_index = (bond_rank * slab_rows + jnp.arange(slab_rows, dtype=jnp.int32)) // BLOCK
    full_index = jnp.arange(bond_width, dtype=jnp.int32) // BLOCK
    charge_left = lookup(left_index, charge_row[0], blocks)
    charge_right = lookup(full_index, charge_row[1], blocks)
    charge_parent = lookup(full_index, charge_row[2], blocks)
    charge_sum = (
        charge_left[:, None, None] + charge_right[None, :, None] - charge_parent[None, None, :]
    )
    keep_mask = jnp.mod(charge_sum, QMOD) == 0
    masked = jnp.where(keep_mask, weight, jnp.zeros((), weight.dtype))
    by_right = lax.all_to_all(masked, "bond", split_axis=1, concat_axis=0, tiled=True)
    take_left = (assign[0] != 1).astype(F32)
    take_right = (assign[0] != 0).astype(F32)
    held_ops = lax.all_gather(leaf_ops[0], "bond", axis=1, tiled=True)
    for level_now in range(1, LEVELS + 1):
        reach_by = 2 ** (level_now - 1)
        left_ops = passed_along(held_ops, "leaf", reach_by)
        left_mixed = jnp.dot(
            left_ops.reshape(op_count * bond_width, bond_width),
            by_right.reshape(bond_width, -1),
            preferred_element_type=F32,
        ).astype(BF16)
        left_mixed = left_mixed.reshape(op_count, -1, bond_width)
        left_part = jnp.einsum(
            "rp,krq->kpq",
            by_right.reshape(-1, bond_width),
            left_mixed,
            preferred_element_type=F32,
        )
        right_mixed = jnp.einsum(
            "kcb,abq->kacq", held_ops, masked, preferred_element_type=F32
        ).astype(BF16)
        right_part = jnp.einsum("acp,kacq->kpq", masked, right_mixed, preferred_element_type=F32)
        partial_sum = take_left[:, None, None] * left_part + take_right[:, None, None] * right_part
        held_ops = lax.psum(partial_sum, "bond").astype(BF16)
    result = lax.dynamic_slice_in_dim(held_ops, bond_rank * slab_rows, slab_rows, 1)
    return result[None]


CHARGES_AT = 2


def fits(info, blocks, left, right, parent):
    total = (
        info[CHARGES_AT + left]
        + info[CHARGES_AT + blocks + right]
        - info[CHARGES_AT + 2 * blocks + parent]
    )
    return lax.rem(total + QMOD, QMOD) == 0


def pieces_ahead(info, blocks, left, right):
    count = jnp.int32(0)
    for k in range(blocks):
        for p in range(blocks):
            count += (fits(info, blocks, left, k, p) & (k < right)).astype(jnp.int32)
    return count


def add_group(op, mats, total):
    count, width = mats.shape[0], mats.shape[1]
    mixed = [dot(op, mats[j], 1, 0).astype(BF16) for j in range(count)]
    return total + dot(
        mats.reshape(count * width, width), jnp.concatenate(mixed, 0), 0, 0
    )


def halves_swapped(x):
    return jnp.concatenate([x[..., BLOCK:], x[..., :BLOCK]], axis=-1)


def pack_kernel(blocks, partners, info, weight, branch, packed, turned, turn):
    k = pl.program_id(0)
    rank = info[0]
    area = GROUP * ROWS
    slab, width = weight.shape[0], weight.shape[-1]
    quarters = slab // GROUP

    @pl.when(k == 0)
    def _():
        to = lax.broadcasted_iota(jnp.int32, (area, area), 0)
        at = lax.broadcasted_iota(jnp.int32, (area, area), 1)
        turn[...] = jnp.where(at == (to % GROUP) * ROWS + to // GROUP, 1.0, 0.0).astype(BF16)
        need = lax.fori_loop(
            0,
            blocks,
            lambda d, most: jnp.maximum(most, pieces_ahead(info, blocks, d, blocks)),
            jnp.int32(0),
        )
        step = jnp.int32(1)
        for cap in CAPACITIES[:-1]:
            step += (need > cap).astype(jnp.int32)
        branch[0] = jnp.where(info[1] == 1, 0, step)

    allowed = [fits(info, blocks, rank, k, p) for p in range(blocks)]
    some = functools.reduce(jnp.logical_or, allowed)

    @pl.when(some & (info[1] != 1))
    def _():
        for m in range(partners):
            for g in range(quarters):
                rows = weight[g * GROUP : (g + 1) * GROUP, rank ^ m].reshape(area, width)
                turned[m, g] = dot(turn[...], rows, 1, 0).astype(BF16)
        slot = pieces_ahead(info, blocks, rank, k)
        for p in range(blocks):

            @pl.when(allowed[p])
            def _():
                lanes = slice(p * BLOCK, (p + 1) * BLOCK)
                for m in range(partners):
                    for h in range(quarters // 2):
                        both = jnp.concatenate(
                            [turned[m, h, :, lanes], turned[m, h + quarters // 2, :, lanes]], axis=1
                        )
                        packed[m, slot, :, h * GROUP : (h + 1) * GROUP, :] = both.reshape(
                            ROWS, GROUP, 2 * BLOCK
                        )

            slot = slot + allowed[p].astype(jnp.int32)


def pack(info, weight):
    slab, width = weight.shape[0], weight.shape[1]
    partners = lax.axis_size("bond")
    blocks = width // BLOCK
    cut = weight.reshape(slab, blocks, partners, ROWS, width)
    whole = (partners, blocks * blocks, ROWS, slab // 2, 2 * BLOCK)
    branch, packed = pl.pallas_call(
        functools.partial(pack_kernel, blocks, partners),
        grid=(blocks,),
        in_specs=[
            SMEM,
            pl.BlockSpec((slab, None, partners, ROWS, width), lambda k: (0, k, 0, 0, 0)),
        ],
        out_specs=[SMEM, VMEM],
        out_shape=[jax.ShapeDtypeStruct((1,), jnp.int32), jax.ShapeDtypeStruct(whole, BF16)],
        scratch_shapes=[
            pltpu.VMEM((partners, slab // GROUP, GROUP * ROWS, width), BF16),
            pltpu.VMEM((GROUP * ROWS, GROUP * ROWS), BF16),
        ],
        compiler_params=pltpu.CompilerParams(vmem_limit_bytes=24 * MIB),
        name="pack",
    )(info, cut)
    return branch[0], packed


def unpack_kernel(partners, info, packed, *rest):
    come, mats = rest[:-1], rest[-1]
    rank = info[0]
    width = mats.shape[-1]
    blocks = width // BLOCK
    half = packed.shape[3]
    lane = lax.broadcasted_iota(jnp.int32, (ROWS, half, 2 * BLOCK), 2)
    low = lane < BLOCK

    for m in range(partners):
        source = rank ^ m

        def take(slot):
            return packed[0, slot] if m == 0 else come[m - 1][slot]

        def step(k, slot):
            for tile in range(blocks // 2):
                first = fits(info, blocks, source, k, 2 * tile)
                second = fits(info, blocks, source, k, 2 * tile + 1)
                last = (packed.shape[1] if m == 0 else come[m - 1].shape[0]) - 1
                after = slot + first.astype(jnp.int32)
                a = take(jnp.minimum(slot, last))
                b = take(jnp.minimum(after, last))
                keep = jnp.where(low, first.astype(jnp.int32), second.astype(jnp.int32)) != 0
                at = pl.multiple_of(source * 2 * half, half)
                rows = pl.ds(pl.multiple_of(k * ROWS, ROWS), ROWS)
                lanes = slice(tile * 2 * BLOCK, (tile + 1) * 2 * BLOCK)
                top = jnp.concatenate([a[..., :BLOCK], b[..., :BLOCK]], axis=-1)
                mats[rows, pl.ds(at, half), lanes] = jnp.where(keep, top, 0)
                low_rows = jnp.concatenate([a[..., BLOCK:], b[..., BLOCK:]], axis=-1)
                mats[rows, pl.ds(at + half, half), lanes] = jnp.where(keep, low_rows, 0)
                slot = after + second.astype(jnp.int32)
            return slot

        lax.fori_loop(0, blocks, step, jnp.int32(0))


def unpack(info, packed, come, width):
    return pl.pallas_call(
        functools.partial(unpack_kernel, packed.shape[0]),
        in_specs=[SMEM, VMEM] + [VMEM] * len(come),
        out_specs=VMEM,
        out_shape=jax.ShapeDtypeStruct((ROWS * (width // BLOCK), width, width), BF16),
        compiler_params=pltpu.CompilerParams(vmem_limit_bytes=32 * MIB),
        name="unpack",
    )(info, packed, *come)


def unset(shape):
    return pl.pallas_call(
        lambda out: None,
        out_specs=VMEM,
        out_shape=jax.ShapeDtypeStruct(shape, BF16),
        compiler_params=pltpu.CompilerParams(vmem_limit_bytes=12 * MIB),
        name="unset",
    )()


def mask_of(info, width):
    blocks = width // BLOCK

    def spread(shape, axis, at):
        block = lax.broadcasted_iota(jnp.int32, shape, axis) // BLOCK
        charge = jnp.zeros(shape, jnp.int32)
        for k in range(blocks):
            charge = jnp.where(block == k, info[at + k], charge)
        return charge

    right = spread((width, width), 0, CHARGES_AT + blocks)
    parent = spread((width, width), 1, CHARGES_AT + 2 * blocks)
    left = info[CHARGES_AT + info[0]]
    return jnp.where(lax.rem(left + right - parent + QMOD, QMOD) == 0, 1.0, 0.0).astype(BF16)


def side_kernel(not_if, masked, per, info, op, before, mats, after):
    after[...] = before[...]

    @pl.when(info[1] != not_if)
    def _():
        mask = mask_of(info, op.shape[0]) if masked else None

        @pl.loop(0, mats.shape[0] // per)
        def _(c):
            group = mats[pl.ds(pl.multiple_of(c * per, per), per)]
            if masked:
                group = group * mask[None]
            after[...] = add_group(op[...], group, after[...])


def side(not_if, info, op, before, mats, masked, per):
    width = op.shape[0]
    total = mats.shape[0]
    return pl.pallas_call(
        functools.partial(side_kernel, not_if, masked, per),
        in_specs=[SMEM, VMEM, VMEM, VMEM],
        out_specs=VMEM,
        out_shape=jax.ShapeDtypeStruct((width, width), F32),
        compiler_params=pltpu.CompilerParams(vmem_limit_bytes=24 * MIB),
        cost_estimate=pl.CostEstimate(
            flops=4 * total * width**3, bytes_accessed=2 * total * width**2, transcendentals=0
        ),
        name="side",
    )(info, op, before, mats)


def shards(isometries, leaf_ops, charges, assign):
    rank = lax.axis_index("bond")
    partners = lax.axis_size("bond")
    weight = isometries[0]
    slab, width = weight.shape[0], weight.shape[1]
    own = leaf_ops[0, 0]
    left = passed_along(own, "leaf", 1)
    info = jnp.concatenate([rank.reshape(1).astype(jnp.int32), assign[0], charges[0].reshape(-1)])
    zeros = jnp.zeros((width, width), F32)

    def gathered(part):
        both = jnp.stack([part] + [swapped(part, m) for m in range(1, partners)])
        return jnp.take(both, jnp.arange(partners) ^ rank, axis=0)

    def ops_of(own, left):
        full = gathered(jnp.stack([own, left]))
        return full[:, 0].reshape(width, width), full[:, 1].reshape(width, width)

    branch, packed = pack(info, weight)

    def without(info, weight, own, left, packed):
        op, left_op = ops_of(own, left)
        total = side(0, info, op, zeros, weight, True, 8)
        return total, left_op, unset((ROWS * (width // BLOCK), width, width))

    def exchange(cap, info, weight, own, left, packed):
        op, left_op = ops_of(own, left)
        come = [swapped(packed[m, :cap], m) for m in range(1, partners)]
        total = side(0, info, op, zeros, weight, True, 8)
        return total, left_op, unpack(info, packed, come, width)

    total, left_op, mats = lax.switch(
        branch,
        [without] + [functools.partial(exchange, cap) for cap in CAPACITIES],
        info, weight, own, left, packed,
    )
    total = side(1, info, left_op, total, mats, False, 32)
    for level in range(2, LEVELS + 1):
        sent = total.astype(BF16)
        come = [swapped(sent, m) for m in range(1, partners)]
        op = (total + sum(c.astype(F32) for c in come)).astype(BF16)
        left_op = passed_along(op, "leaf", 2 ** (level - 1))
        total = side(0, info, op, zeros, weight, True, 32)
        total = side(1, info, left_op, total, mats, False, 32)

    def rows_of(m):
        return lax.dynamic_slice_in_dim(total, (rank ^ m) * slab, slab, 0)

    result = rows_of(0)
    for m in range(1, partners):
        result = result + swapped(rows_of(m), m)
    return result.astype(BF16)[None, None]


def solution(mesh):
    in_specs = (
        P("leaf", "bond", None, None),
        P("leaf", None, "bond", None),
        P("leaf", None, None),
        P("leaf", None),
    )
    out_specs = P("leaf", None, "bond", None)
    partners = mesh.shape["bond"]

    def whole(isometries, leaf_ops, charges, assign):
        width = isometries.shape[1]
        fits = (
            partners & (partners - 1) == 0
            and width // partners == BLOCK
            and BLOCK == partners * ROWS
            and charges.shape[2] * BLOCK == width
            and leaf_ops.shape[1] == 1
        )
        return jax.shard_map(
            shards if fits else shards_plain,
            mesh=mesh, in_specs=in_specs, out_specs=out_specs, check_vma=False,
        )(isometries, leaf_ops, charges, assign)

    return whole
```

```python
import functools

import jax
import jax.numpy as jnp
from jax import lax
from jax.experimental import pallas as pl
from jax.experimental.pallas import tpu as pltpu
from jax.sharding import PartitionSpec as P

BLOCK = 64
QMOD = 4
LEVELS = 3
ROWS = 16
GROUP = 16
CAPACITIES = (4, 6, 8, 10, 12, 16)
F32 = jnp.float32
BF16 = jnp.bfloat16
MIB = 2**20
ANY = pl.BlockSpec(memory_space=pl.ANY)
VMEM = pl.BlockSpec(memory_space=pltpu.VMEM)
SMEM = pl.BlockSpec(memory_space=pltpu.SMEM)


def dot(a, b, ca, cb):
    return lax.dot_general(a, b, (((ca,), (cb,)), ((), ())), preferred_element_type=F32)


def passed_along(array, axis, by):
    devices = lax.axis_size(axis)
    return lax.ppermute(array, axis, [(i, (i + by) % devices) for i in range(devices)])


def swapped(array, mask):
    devices = lax.axis_size("bond")
    return lax.ppermute(array, "bond", [(i, i ^ mask) for i in range(devices)])


def lookup(index_vector, charge_table, blocks):
    hits = index_vector[:, None] == blocks[None, :]
    return jnp.sum(jnp.where(hits, charge_table[None, :], 0), axis=1)


def shards_plain(isometries, leaf_ops, charges, assign):
    bond_rank = lax.axis_index("bond")
    weight = isometries[0]
    slab_rows = weight.shape[0]
    bond_width = weight.shape[1]
    op_count = leaf_ops.shape[1]
    charge_row = charges[0]
    blocks = jnp.arange(charge_row.shape[1], dtype=jnp.int32)
    left_index = (bond_rank * slab_rows + jnp.arange(slab_rows, dtype=jnp.int32)) // BLOCK
    full_index = jnp.arange(bond_width, dtype=jnp.int32) // BLOCK
    charge_left = lookup(left_index, charge_row[0], blocks)
    charge_right = lookup(full_index, charge_row[1], blocks)
    charge_parent = lookup(full_index, charge_row[2], blocks)
    charge_sum = (
        charge_left[:, None, None] + charge_right[None, :, None] - charge_parent[None, None, :]
    )
    keep_mask = jnp.mod(charge_sum, QMOD) == 0
    masked = jnp.where(keep_mask, weight, jnp.zeros((), weight.dtype))
    by_right = lax.all_to_all(masked, "bond", split_axis=1, concat_axis=0, tiled=True)
    take_left = (assign[0] != 1).astype(F32)
    take_right = (assign[0] != 0).astype(F32)
    held_ops = lax.all_gather(leaf_ops[0], "bond", axis=1, tiled=True)
    for level_now in range(1, LEVELS + 1):
        reach_by = 2 ** (level_now - 1)
        left_ops = passed_along(held_ops, "leaf", reach_by)
        left_mixed = jnp.dot(
            left_ops.reshape(op_count * bond_width, bond_width),
            by_right.reshape(bond_width, -1),
            preferred_element_type=F32,
        ).astype(BF16)
        left_mixed = left_mixed.reshape(op_count, -1, bond_width)
        left_part = jnp.einsum(
            "rp,krq->kpq",
            by_right.reshape(-1, bond_width),
            left_mixed,
            preferred_element_type=F32,
        )
        right_mixed = jnp.einsum(
            "kcb,abq->kacq", held_ops, masked, preferred_element_type=F32
        ).astype(BF16)
        right_part = jnp.einsum("acp,kacq->kpq", masked, right_mixed, preferred_element_type=F32)
        partial_sum = take_left[:, None, None] * left_part + take_right[:, None, None] * right_part
        held_ops = lax.psum(partial_sum, "bond").astype(BF16)
    result = lax.dynamic_slice_in_dim(held_ops, bond_rank * slab_rows, slab_rows, 1)
    return result[None]


CHARGES_AT = 2


def fits(info, blocks, left, right, parent):
    total = (
        info[CHARGES_AT + left]
        + info[CHARGES_AT + blocks + right]
        - info[CHARGES_AT + 2 * blocks + parent]
    )
    return lax.rem(total + QMOD, QMOD) == 0


def pieces_ahead(info, blocks, left, right):
    count = jnp.int32(0)
    for k in range(blocks):
        for p in range(blocks):
            count += (fits(info, blocks, left, k, p) & (k < right)).astype(jnp.int32)
    return count


def add_group(op, mats, total):
    count, width = mats.shape[0], mats.shape[1]
    mixed = [dot(op, mats[j], 1, 0).astype(BF16) for j in range(count)]
    return total + dot(
        mats.reshape(count * width, width), jnp.concatenate(mixed, 0), 0, 0
    )


def halves_swapped(x):
    return jnp.concatenate([x[..., BLOCK:], x[..., :BLOCK]], axis=-1)


def pack_kernel(blocks, partners, info, weight, branch, own, *rest):
    groups = len(CAPACITIES)
    sends = rest[: groups * (partners - 1)]
    stage, turned, turn, sems = rest[groups * (partners - 1) :]
    k = pl.program_id(0)
    rank = info[0]
    area = GROUP * ROWS
    slab, width = weight.shape[0], weight.shape[-1]
    quarters = slab // GROUP

    @pl.when(k == 0)
    def _():
        to = lax.broadcasted_iota(jnp.int32, (area, area), 0)
        at = lax.broadcasted_iota(jnp.int32, (area, area), 1)
        turn[...] = jnp.where(at == (to % GROUP) * ROWS + to // GROUP, 1.0, 0.0).astype(BF16)
        need = lax.fori_loop(
            0,
            blocks,
            lambda d, most: jnp.maximum(most, pieces_ahead(info, blocks, d, blocks)),
            jnp.int32(0),
        )
        step = jnp.int32(1)
        for cap in CAPACITIES[:-1]:
            step += (need > cap).astype(jnp.int32)
        branch[0] = jnp.where(info[1] == 1, 0, step)

    allowed = [fits(info, blocks, rank, k, p) for p in range(blocks)]
    some = functools.reduce(jnp.logical_or, allowed)

    @pl.when(some & (info[1] != 1))
    def _():
        for m in range(partners):
            for g in range(quarters):
                rows = weight[g * GROUP : (g + 1) * GROUP, rank ^ m].reshape(area, width)
                turned[m, g] = dot(turn[...], rows, 1, 0).astype(BF16)
        slot = pieces_ahead(info, blocks, rank, k)
        for p in range(blocks):

            @pl.when(allowed[p])
            def _():
                lanes = slice(p * BLOCK, (p + 1) * BLOCK)
                for m in range(partners):
                    for h in range(quarters // 2):
                        both = jnp.concatenate(
                            [turned[m, h, :, lanes], turned[m, h + quarters // 2, :, lanes]], axis=1
                        )
                        stage[m, slot, :, h * GROUP : (h + 1) * GROUP, :] = both.reshape(
                            ROWS, GROUP, 2 * BLOCK
                        )

            slot = slot + allowed[p].astype(jnp.int32)

    @pl.when(k == blocks - 1)
    def _():
        for g, cap in enumerate(CAPACITIES):

            @pl.when(branch[0] == g + 1)
            def _():
                copies = []
                for m in range(partners):
                    to = sends[g * (partners - 1) + m - 1] if m else own.at[pl.ds(0, cap)]
                    copies.append(
                        pltpu.make_async_copy(stage.at[m, pl.ds(0, cap)], to, sems.at[m])
                    )
                for copy in copies:
                    copy.start()
                for copy in copies:
                    copy.wait()


def pack(info, weight):
    slab, width = weight.shape[0], weight.shape[1]
    partners = lax.axis_size("bond")
    blocks = width // BLOCK
    cut = weight.reshape(slab, blocks, partners, ROWS, width)
    piece = (ROWS, slab // 2, 2 * BLOCK)
    most = blocks * blocks
    sends = [jax.ShapeDtypeStruct((cap,) + piece, BF16) for cap in CAPACITIES for _ in range(1, partners)]
    branch, own, *packed = pl.pallas_call(
        functools.partial(pack_kernel, blocks, partners),
        grid=(blocks,),
        in_specs=[
            SMEM,
            pl.BlockSpec((slab, None, partners, ROWS, width), lambda k: (0, k, 0, 0, 0)),
        ],
        out_specs=[SMEM, ANY] + [ANY] * len(sends),
        out_shape=[
            jax.ShapeDtypeStruct((1,), jnp.int32),
            jax.ShapeDtypeStruct((most,) + piece, BF16),
        ]
        + sends,
        scratch_shapes=[
            pltpu.VMEM((partners, most) + piece, BF16),
            pltpu.VMEM((partners, slab // GROUP, GROUP * ROWS, width), BF16),
            pltpu.VMEM((GROUP * ROWS, GROUP * ROWS), BF16),
            pltpu.SemaphoreType.DMA((partners,)),
        ],
        compiler_params=pltpu.CompilerParams(vmem_limit_bytes=24 * MIB),
        name="pack",
    )(info, cut)
    each = partners - 1
    return branch[0], own, [packed[g * each : (g + 1) * each] for g in range(len(CAPACITIES))]


def unpack_kernel(partners, info, own, *rest):
    come, out, mats, sems = rest[: partners - 1], rest[-3], rest[-2], rest[-1]
    rank = info[0]
    width = mats.shape[-1]
    blocks = width // BLOCK
    half = own.shape[2]
    lane = lax.broadcasted_iota(jnp.int32, (ROWS, half, 2 * BLOCK), 2)
    low = lane < BLOCK

    def leave(k):
        rows = pl.ds(pl.multiple_of(k * ROWS, ROWS), ROWS)
        return pltpu.make_async_copy(mats.at[rows], out.at[rows], sems.at[k])

    def step(k, slots):
        rows = pl.ds(pl.multiple_of(k * ROWS, ROWS), ROWS)
        after = []
        for m in range(partners):
            source = rank ^ m
            pieces = come[m - 1] if m else own
            last = pieces.shape[0] - 1
            slot = slots[m]
            for tile in range(blocks // 2):
                first = fits(info, blocks, source, k, 2 * tile)
                second = fits(info, blocks, source, k, 2 * tile + 1)
                middle = slot + first.astype(jnp.int32)
                a = pieces[jnp.minimum(slot, last)]
                b = pieces[jnp.minimum(middle, last)]
                keep = jnp.where(low, first.astype(jnp.int32), second.astype(jnp.int32)) != 0
                at = pl.multiple_of(source * 2 * half, half)
                lanes = slice(tile * 2 * BLOCK, (tile + 1) * 2 * BLOCK)
                upper = jnp.concatenate([a[..., :BLOCK], b[..., :BLOCK]], axis=-1)
                mats[rows, pl.ds(at, half), lanes] = jnp.where(keep, upper, 0)
                lower = jnp.concatenate([a[..., BLOCK:], b[..., BLOCK:]], axis=-1)
                mats[rows, pl.ds(at + half, half), lanes] = jnp.where(keep, lower, 0)
                slot = middle + second.astype(jnp.int32)
            after.append(slot)
        leave(k).start()
        return tuple(after)

    lax.fori_loop(0, blocks, step, (jnp.int32(0),) * partners)

    @pl.loop(0, blocks)
    def _(k):
        leave(k).wait()


def unpack(info, own, come, width):
    blocks = width // BLOCK
    whole = (ROWS * blocks, width, width)
    return pl.pallas_call(
        functools.partial(unpack_kernel, len(come) + 1),
        in_specs=[SMEM, VMEM] + [VMEM] * len(come),
        out_specs=ANY,
        out_shape=jax.ShapeDtypeStruct(whole, BF16),
        scratch_shapes=[pltpu.VMEM(whole, BF16), pltpu.SemaphoreType.DMA((blocks,))],
        compiler_params=pltpu.CompilerParams(vmem_limit_bytes=24 * MIB),
        name="unpack",
    )(info, own, *come)


def unset(shape):
    return pl.pallas_call(
        lambda out: None,
        out_specs=ANY,
        out_shape=jax.ShapeDtypeStruct(shape, BF16),
        name="unset",
    )()


def mask_of(info, width):
    blocks = width // BLOCK

    def spread(shape, axis, at):
        block = lax.broadcasted_iota(jnp.int32, shape, axis) // BLOCK
        charge = jnp.zeros(shape, jnp.int32)
        for k in range(blocks):
            charge = jnp.where(block == k, info[at + k], charge)
        return charge

    right = spread((width, width), 0, CHARGES_AT + blocks)
    parent = spread((width, width), 1, CHARGES_AT + 2 * blocks)
    left = info[CHARGES_AT + info[0]]
    return jnp.where(lax.rem(left + right - parent + QMOD, QMOD) == 0, 1.0, 0.0).astype(BF16)


def side_kernel(not_if, masked, sizes, quarters, info, before, mats, *rest):
    ops, (after, held, whole, sems) = rest[:quarters], rest[quarters:]
    after[...] = before[...]
    rows = ops[0].shape[0]
    starts = [sum(sizes[:c]) for c in range(len(sizes))]

    def load(c):
        part = pl.ds(starts[c], sizes[c])
        return pltpu.make_async_copy(mats.at[part], held.at[part], sems.at[c])

    @pl.when(info[1] != not_if)
    def _():
        for c in range(len(sizes)):
            load(c).start()
        mask = mask_of(info, whole.shape[0]) if masked else None
        for m in range(quarters if quarters > 1 else 0):
            whole[pl.ds(pl.multiple_of((info[0] ^ m) * rows, rows), rows)] = ops[m][...]
        op = whole if quarters > 1 else ops[0]

        def add(group):
            if masked:
                group = group * mask[None]
            after[...] = add_group(op[...], group, after[...])

        if len(set(sizes)) == 1:
            size = sizes[0]

            @pl.loop(0, len(sizes))
            def _(c):
                part = pl.ds(pl.multiple_of(c * size, size), size)
                pltpu.make_async_copy(mats.at[part], held.at[part], sems.at[c]).wait()
                add(held[part])
        else:
            for c in range(len(sizes)):
                load(c).wait()
                add(held[starts[c] : starts[c] + sizes[c]])


def side(not_if, info, op, before, mats, masked, sizes):
    width = mats.shape[-1]
    total = mats.shape[0]
    ops = op if isinstance(op, (list, tuple)) else [op]
    return pl.pallas_call(
        functools.partial(side_kernel, not_if, masked, sizes, len(ops)),
        in_specs=[SMEM, VMEM, ANY] + [VMEM] * len(ops),
        out_specs=VMEM,
        out_shape=jax.ShapeDtypeStruct((width, width), F32),
        scratch_shapes=[
            pltpu.VMEM((total, width, width), BF16),
            pltpu.VMEM((width, width), BF16),
            pltpu.SemaphoreType.DMA((len(sizes),)),
        ],
        compiler_params=pltpu.CompilerParams(vmem_limit_bytes=28 * MIB),
        cost_estimate=pl.CostEstimate(
            flops=4 * total * width**3, bytes_accessed=2 * total * width**2, transcendentals=0
        ),
        name="side",
    )(info, before, mats, *ops)


def rolled(total):
    return (total // 8,) * 8


def fast(total):
    return (total // 8, 3 * total // 8, total // 2)


def shards(isometries, leaf_ops, charges, assign):
    rank = lax.axis_index("bond")
    partners = lax.axis_size("bond")
    weight = isometries[0]
    slab, width = weight.shape[0], weight.shape[1]
    own = leaf_ops[0, 0]
    left = passed_along(own, "leaf", 1)
    info = jnp.concatenate([rank.reshape(1).astype(jnp.int32), assign[0], charges[0].reshape(-1)])
    zeros = jnp.zeros((width, width), F32)

    def gathered(part):
        return [part] + [swapped(part, m) for m in range(1, partners)]

    op = gathered(own)
    branch, mine, packed = pack(info, weight)

    def without(info, weight, op, left, mine, packed):
        total = side(0, info, op, zeros, weight, True, rolled(slab))
        return total, [left] * partners, unset((ROWS * (width // BLOCK), width, width))

    def exchange(g, info, weight, op, left, mine, packed):
        come = [swapped(packed[g][m - 1], m) for m in range(1, partners)]
        total = side(0, info, op, zeros, weight, True, rolled(slab))
        left, total = lax.optimization_barrier((left, total))
        left_op = gathered(left)
        return total, left_op, unpack(info, mine, come, width)

    total, left_op, mats = lax.switch(
        branch,
        [without] + [functools.partial(exchange, g) for g in range(len(CAPACITIES))],
        info, weight, op, left, mine, packed,
    )
    count = mats.shape[0]
    total = side(1, info, left_op, total, mats, False, fast(count))
    for level in range(2, LEVELS + 1):
        sent = total.astype(BF16)
        come = [swapped(sent, m) for m in range(1, partners)]
        op = (total + sum(c.astype(F32) for c in come)).astype(BF16)
        left_op = passed_along(op, "leaf", 2 ** (level - 1))
        total = side(0, info, op, zeros, weight, True, fast(slab))
        total = side(1, info, left_op, total, mats, False, fast(count))

    def rows_of(m):
        return lax.dynamic_slice_in_dim(total, (rank ^ m) * slab, slab, 0)

    result = rows_of(0)
    for m in range(1, partners):
        result = result + swapped(rows_of(m), m)
    return result.astype(BF16)[None, None]


def solution(mesh):
    in_specs = (
        P("leaf", "bond", None, None),
        P("leaf", None, "bond", None),
        P("leaf", None, None),
        P("leaf", None),
    )
    out_specs = P("leaf", None, "bond", None)
    partners = mesh.shape["bond"]

    def whole(isometries, leaf_ops, charges, assign):
        width = isometries.shape[1]
        fits = (
            partners & (partners - 1) == 0
            and width // partners == BLOCK
            and BLOCK == partners * ROWS
            and charges.shape[2] * BLOCK == width
            and leaf_ops.shape[1] == 1
        )
        return jax.shard_map(
            shards if fits else shards_plain,
            mesh=mesh, in_specs=in_specs, out_specs=out_specs, check_vma=False,
        )(isometries, leaf_ops, charges, assign)

    return whole
```

```python
import functools

import jax
import jax.numpy as jnp
from jax import lax
from jax.experimental import pallas as pl
from jax.experimental.pallas import tpu as pltpu
from jax.sharding import PartitionSpec as P

BLOCK = 64
QMOD = 4
LEVELS = 3
ROWS = 16
GROUP = 16
CAPACITIES = (4, 6, 8, 10, 12, 16)
F32 = jnp.float32
BF16 = jnp.bfloat16
MIB = 2**20
ANY = pl.BlockSpec(memory_space=pl.ANY)
VMEM = pl.BlockSpec(memory_space=pltpu.VMEM)
SMEM = pl.BlockSpec(memory_space=pltpu.SMEM)


def dot(a, b, ca, cb):
    return lax.dot_general(a, b, (((ca,), (cb,)), ((), ())), preferred_element_type=F32)


def passed_along(array, axis, by):
    devices = lax.axis_size(axis)
    return lax.ppermute(array, axis, [(i, (i + by) % devices) for i in range(devices)])


def swapped(array, mask):
    devices = lax.axis_size("bond")
    return lax.ppermute(array, "bond", [(i, i ^ mask) for i in range(devices)])


def lookup(index_vector, charge_table, blocks):
    hits = index_vector[:, None] == blocks[None, :]
    return jnp.sum(jnp.where(hits, charge_table[None, :], 0), axis=1)


def shards_plain(isometries, leaf_ops, charges, assign):
    bond_rank = lax.axis_index("bond")
    weight = isometries[0]
    slab_rows = weight.shape[0]
    bond_width = weight.shape[1]
    op_count = leaf_ops.shape[1]
    charge_row = charges[0]
    blocks = jnp.arange(charge_row.shape[1], dtype=jnp.int32)
    left_index = (bond_rank * slab_rows + jnp.arange(slab_rows, dtype=jnp.int32)) // BLOCK
    full_index = jnp.arange(bond_width, dtype=jnp.int32) // BLOCK
    charge_left = lookup(left_index, charge_row[0], blocks)
    charge_right = lookup(full_index, charge_row[1], blocks)
    charge_parent = lookup(full_index, charge_row[2], blocks)
    charge_sum = (
        charge_left[:, None, None] + charge_right[None, :, None] - charge_parent[None, None, :]
    )
    keep_mask = jnp.mod(charge_sum, QMOD) == 0
    masked = jnp.where(keep_mask, weight, jnp.zeros((), weight.dtype))
    by_right = lax.all_to_all(masked, "bond", split_axis=1, concat_axis=0, tiled=True)
    take_left = (assign[0] != 1).astype(F32)
    take_right = (assign[0] != 0).astype(F32)
    held_ops = lax.all_gather(leaf_ops[0], "bond", axis=1, tiled=True)
    for level_now in range(1, LEVELS + 1):
        reach_by = 2 ** (level_now - 1)
        left_ops = passed_along(held_ops, "leaf", reach_by)
        left_mixed = jnp.dot(
            left_ops.reshape(op_count * bond_width, bond_width),
            by_right.reshape(bond_width, -1),
            preferred_element_type=F32,
        ).astype(BF16)
        left_mixed = left_mixed.reshape(op_count, -1, bond_width)
        left_part = jnp.einsum(
            "rp,krq->kpq",
            by_right.reshape(-1, bond_width),
            left_mixed,
            preferred_element_type=F32,
        )
        right_mixed = jnp.einsum(
            "kcb,abq->kacq", held_ops, masked, preferred_element_type=F32
        ).astype(BF16)
        right_part = jnp.einsum("acp,kacq->kpq", masked, right_mixed, preferred_element_type=F32)
        partial_sum = take_left[:, None, None] * left_part + take_right[:, None, None] * right_part
        held_ops = lax.psum(partial_sum, "bond").astype(BF16)
    result = lax.dynamic_slice_in_dim(held_ops, bond_rank * slab_rows, slab_rows, 1)
    return result[None]


CHARGES_AT = 2


def fits(info, blocks, left, right, parent):
    total = (
        info[CHARGES_AT + left]
        + info[CHARGES_AT + blocks + right]
        - info[CHARGES_AT + 2 * blocks + parent]
    )
    return lax.rem(total + QMOD, QMOD) == 0


def pieces_ahead(info, blocks, left, right):
    count = jnp.int32(0)
    for k in range(blocks):
        for p in range(blocks):
            count += (fits(info, blocks, left, k, p) & (k < right)).astype(jnp.int32)
    return count


def add_group(op, mats, total):
    count, width = mats.shape[0], mats.shape[1]
    mixed = [dot(op, mats[j], 1, 0).astype(BF16) for j in range(count)]
    return total + dot(
        mats.reshape(count * width, width), jnp.concatenate(mixed, 0), 0, 0
    )


def halves_swapped(x):
    return jnp.concatenate([x[..., BLOCK:], x[..., :BLOCK]], axis=-1)


def pack_kernel(blocks, partners, info, weight, branch, own, *rest):
    groups = len(CAPACITIES)
    sends = rest[: groups * (partners - 1)]
    stage, turned, turn, sems = rest[groups * (partners - 1) :]
    k = pl.program_id(0)
    rank = info[0]
    area = GROUP * ROWS
    slab, width = weight.shape[0], weight.shape[-1]
    quarters = slab // GROUP

    @pl.when(k == 0)
    def _():
        to = lax.broadcasted_iota(jnp.int32, (area, area), 0)
        at = lax.broadcasted_iota(jnp.int32, (area, area), 1)
        turn[...] = jnp.where(at == (to % GROUP) * ROWS + to // GROUP, 1.0, 0.0).astype(BF16)
        need = lax.fori_loop(
            0,
            blocks,
            lambda d, most: jnp.maximum(most, pieces_ahead(info, blocks, d, blocks)),
            jnp.int32(0),
        )
        step = jnp.int32(1)
        for cap in CAPACITIES[:-1]:
            step += (need > cap).astype(jnp.int32)
        branch[0] = jnp.where(info[1] == 1, 0, step)

    allowed = [fits(info, blocks, rank, k, p) for p in range(blocks)]
    some = functools.reduce(jnp.logical_or, allowed)

    @pl.when(some & (info[1] != 1))
    def _():
        for m in range(partners):
            for g in range(quarters):
                rows = weight[g * GROUP : (g + 1) * GROUP, rank ^ m].reshape(area, width)
                turned[m, g] = dot(turn[...], rows, 1, 0).astype(BF16)
        slot = pieces_ahead(info, blocks, rank, k)
        for p in range(blocks):

            @pl.when(allowed[p])
            def _():
                lanes = slice(p * BLOCK, (p + 1) * BLOCK)
                for m in range(partners):
                    for h in range(quarters // 2):
                        both = jnp.concatenate(
                            [turned[m, h, :, lanes], turned[m, h + quarters // 2, :, lanes]], axis=1
                        )
                        stage[m, slot, :, h * GROUP : (h + 1) * GROUP, :] = both.reshape(
                            ROWS, GROUP, 2 * BLOCK
                        )

            slot = slot + allowed[p].astype(jnp.int32)

    @pl.when(k == blocks - 1)
    def _():
        for g, cap in enumerate(CAPACITIES):

            @pl.when(branch[0] == g + 1)
            def _():
                copies = []
                for m in range(partners):
                    to = sends[g * (partners - 1) + m - 1] if m else own.at[pl.ds(0, cap)]
                    copies.append(
                        pltpu.make_async_copy(stage.at[m, pl.ds(0, cap)], to, sems.at[m])
                    )
                for copy in copies:
                    copy.start()
                for copy in copies:
                    copy.wait()


def pack(info, weight):
    slab, width = weight.shape[0], weight.shape[1]
    partners = lax.axis_size("bond")
    blocks = width // BLOCK
    cut = weight.reshape(slab, blocks, partners, ROWS, width)
    piece = (ROWS, slab // 2, 2 * BLOCK)
    most = blocks * blocks
    sends = [jax.ShapeDtypeStruct((cap,) + piece, BF16) for cap in CAPACITIES for _ in range(1, partners)]
    branch, own, *packed = pl.pallas_call(
        functools.partial(pack_kernel, blocks, partners),
        grid=(blocks,),
        in_specs=[
            SMEM,
            pl.BlockSpec((slab, None, partners, ROWS, width), lambda k: (0, k, 0, 0, 0)),
        ],
        out_specs=[SMEM, ANY] + [ANY] * len(sends),
        out_shape=[
            jax.ShapeDtypeStruct((1,), jnp.int32),
            jax.ShapeDtypeStruct((most,) + piece, BF16),
        ]
        + sends,
        scratch_shapes=[
            pltpu.VMEM((partners, most) + piece, BF16),
            pltpu.VMEM((partners, slab // GROUP, GROUP * ROWS, width), BF16),
            pltpu.VMEM((GROUP * ROWS, GROUP * ROWS), BF16),
            pltpu.SemaphoreType.DMA((partners,)),
        ],
        compiler_params=pltpu.CompilerParams(vmem_limit_bytes=24 * MIB),
        name="pack",
    )(info, cut)
    each = partners - 1
    return branch[0], own, [packed[g * each : (g + 1) * each] for g in range(len(CAPACITIES))]


def unpack_kernel(partners, info, own, *rest):
    come, out, mats, sems = rest[: partners - 1], rest[-3], rest[-2], rest[-1]
    rank = info[0]
    width = mats.shape[-1]
    blocks = width // BLOCK
    half = own.shape[2]
    lane = lax.broadcasted_iota(jnp.int32, (ROWS, half, 2 * BLOCK), 2)
    low = lane < BLOCK

    def leave(k):
        rows = pl.ds(pl.multiple_of(k * ROWS, ROWS), ROWS)
        return pltpu.make_async_copy(mats.at[rows], out.at[rows], sems.at[k])

    def step(k, slots):
        rows = pl.ds(pl.multiple_of(k * ROWS, ROWS), ROWS)
        after = []
        for m in range(partners):
            source = rank ^ m
            pieces = come[m - 1] if m else own
            last = pieces.shape[0] - 1
            slot = slots[m]
            for tile in range(blocks // 2):
                first = fits(info, blocks, source, k, 2 * tile)
                second = fits(info, blocks, source, k, 2 * tile + 1)
                middle = slot + first.astype(jnp.int32)
                a = pieces[jnp.minimum(slot, last)]
                b = pieces[jnp.minimum(middle, last)]
                keep = jnp.where(low, first.astype(jnp.int32), second.astype(jnp.int32)) != 0
                at = pl.multiple_of(source * 2 * half, half)
                lanes = slice(tile * 2 * BLOCK, (tile + 1) * 2 * BLOCK)
                upper = jnp.concatenate([a[..., :BLOCK], b[..., :BLOCK]], axis=-1)
                mats[rows, pl.ds(at, half), lanes] = jnp.where(keep, upper, 0)
                lower = jnp.concatenate([a[..., BLOCK:], b[..., BLOCK:]], axis=-1)
                mats[rows, pl.ds(at + half, half), lanes] = jnp.where(keep, lower, 0)
                slot = middle + second.astype(jnp.int32)
            after.append(slot)
        leave(k).start()
        return tuple(after)

    lax.fori_loop(0, blocks, step, (jnp.int32(0),) * partners)

    @pl.loop(0, blocks)
    def _(k):
        leave(k).wait()


def unpack(info, own, come, width):
    blocks = width // BLOCK
    whole = (ROWS * blocks, width, width)
    return pl.pallas_call(
        functools.partial(unpack_kernel, len(come) + 1),
        in_specs=[SMEM, VMEM] + [VMEM] * len(come),
        out_specs=ANY,
        out_shape=jax.ShapeDtypeStruct(whole, BF16),
        scratch_shapes=[pltpu.VMEM(whole, BF16), pltpu.SemaphoreType.DMA((blocks,))],
        compiler_params=pltpu.CompilerParams(vmem_limit_bytes=24 * MIB),
        name="unpack",
    )(info, own, *come)


def unset(shape):
    return pl.pallas_call(
        lambda out: None,
        out_specs=ANY,
        out_shape=jax.ShapeDtypeStruct(shape, BF16),
        name="unset",
    )()


def mask_of(info, width):
    blocks = width // BLOCK

    def spread(shape, axis, at):
        block = lax.broadcasted_iota(jnp.int32, shape, axis) // BLOCK
        charge = jnp.zeros(shape, jnp.int32)
        for k in range(blocks):
            charge = jnp.where(block == k, info[at + k], charge)
        return charge

    right = spread((width, width), 0, CHARGES_AT + blocks)
    parent = spread((width, width), 1, CHARGES_AT + 2 * blocks)
    left = info[CHARGES_AT + info[0]]
    return jnp.where(lax.rem(left + right - parent + QMOD, QMOD) == 0, 1.0, 0.0).astype(BF16)


def side_kernel(not_if, masked, sizes, quarters, info, before, mats, *rest):
    ops, (after, held, whole, sems) = rest[:quarters], rest[quarters:]
    after[...] = before[...]
    rows = ops[0].shape[0]
    starts = [sum(sizes[:c]) for c in range(len(sizes))]

    def load(c):
        part = pl.ds(starts[c], sizes[c])
        return pltpu.make_async_copy(mats.at[part], held.at[part], sems.at[c])

    @pl.when(info[1] != not_if)
    def _():
        for c in range(len(sizes)):
            load(c).start()
        mask = mask_of(info, whole.shape[0]) if masked else None
        for m in range(quarters if quarters > 1 else 0):
            whole[pl.ds(pl.multiple_of((info[0] ^ m) * rows, rows), rows)] = ops[m][...]
        op = whole if quarters > 1 else ops[0]

        def add(group):
            if masked:
                group = group * mask[None]
            after[...] = add_group(op[...], group, after[...])

        if len(set(sizes)) == 1:
            size = sizes[0]

            @pl.loop(0, len(sizes))
            def _(c):
                part = pl.ds(pl.multiple_of(c * size, size), size)
                pltpu.make_async_copy(mats.at[part], held.at[part], sems.at[c]).wait()
                add(held[part])
        else:
            for c in range(len(sizes)):
                load(c).wait()
                add(held[starts[c] : starts[c] + sizes[c]])


def side(not_if, info, op, before, mats, masked, sizes):
    width = mats.shape[-1]
    total = mats.shape[0]
    ops = op if isinstance(op, (list, tuple)) else [op]
    return pl.pallas_call(
        functools.partial(side_kernel, not_if, masked, sizes, len(ops)),
        in_specs=[SMEM, VMEM, ANY] + [VMEM] * len(ops),
        out_specs=VMEM,
        out_shape=jax.ShapeDtypeStruct((width, width), F32),
        scratch_shapes=[
            pltpu.VMEM((total, width, width), BF16),
            pltpu.VMEM((width, width), BF16),
            pltpu.SemaphoreType.DMA((len(sizes),)),
        ],
        compiler_params=pltpu.CompilerParams(vmem_limit_bytes=28 * MIB),
        cost_estimate=pl.CostEstimate(
            flops=4 * total * width**3, bytes_accessed=2 * total * width**2, transcendentals=0
        ),
        name="side",
    )(info, before, mats, *ops)


def rolled(total):
    return (total // 8,) * 8


def fast(total):
    return (total // 2,) * 2


def shards(isometries, leaf_ops, charges, assign):
    rank = lax.axis_index("bond")
    partners = lax.axis_size("bond")
    weight = isometries[0]
    slab, width = weight.shape[0], weight.shape[1]
    own = leaf_ops[0, 0]
    left = passed_along(own, "leaf", 1)
    info = jnp.concatenate([rank.reshape(1).astype(jnp.int32), assign[0], charges[0].reshape(-1)])
    zeros = jnp.zeros((width, width), F32)

    def gathered(part):
        return [part] + [swapped(part, m) for m in range(1, partners)]

    op = gathered(own)
    branch, mine, packed = pack(info, weight)

    def without(info, weight, op, left, mine, packed):
        total = side(0, info, op, zeros, weight, True, rolled(slab))
        return total, [left] * partners, unset((ROWS * (width // BLOCK), width, width))

    def exchange(g, info, weight, op, left, mine, packed):
        come = [swapped(packed[g][m - 1], m) for m in range(1, partners)]
        total = side(0, info, op, zeros, weight, True, rolled(slab))
        left, total = lax.optimization_barrier((left, total))
        left_op = gathered(left)
        return total, left_op, unpack(info, mine, come, width)

    total, left_op, mats = lax.switch(
        branch,
        [without] + [functools.partial(exchange, g) for g in range(len(CAPACITIES))],
        info, weight, op, left, mine, packed,
    )
    count = mats.shape[0]
    total = side(1, info, left_op, total, mats, False, fast(count))
    for level in range(2, LEVELS + 1):
        sent = total.astype(BF16)
        come = [swapped(sent, m) for m in range(1, partners)]
        op = (total + sum(c.astype(F32) for c in come)).astype(BF16)
        left_op = passed_along(op, "leaf", 2 ** (level - 1))
        total = side(0, info, op, zeros, weight, True, fast(slab))
        total = side(1, info, left_op, total, mats, False, fast(count))

    def rows_of(m):
        return lax.dynamic_slice_in_dim(total, (rank ^ m) * slab, slab, 0)

    result = rows_of(0)
    for m in range(1, partners):
        result = result + swapped(rows_of(m), m)
    return result.astype(BF16)[None, None]


def solution(mesh):
    in_specs = (
        P("leaf", "bond", None, None),
        P("leaf", None, "bond", None),
        P("leaf", None, None),
        P("leaf", None),
    )
    out_specs = P("leaf", None, "bond", None)
    partners = mesh.shape["bond"]

    def whole(isometries, leaf_ops, charges, assign):
        width = isometries.shape[1]
        fits = (
            partners & (partners - 1) == 0
            and width // partners == BLOCK
            and BLOCK == partners * ROWS
            and charges.shape[2] * BLOCK == width
            and leaf_ops.shape[1] == 1
        )
        return jax.shard_map(
            shards if fits else shards_plain,
            mesh=mesh, in_specs=in_specs, out_specs=out_specs, check_vma=False,
        )(isometries, leaf_ops, charges, assign)

    return whole
```

```python
import functools

import jax
import jax.numpy as jnp
from jax import lax
from jax.experimental import pallas as pl
from jax.experimental.pallas import tpu as pltpu
from jax.sharding import PartitionSpec as P

BLOCK = 64
QMOD = 4
LEVELS = 3
ROWS = 16
GROUP = 16
CAPACITIES = (5, 6, 7, 8, 10, 16)
F32 = jnp.float32
BF16 = jnp.bfloat16
MIB = 2**20
ANY = pl.BlockSpec(memory_space=pl.ANY)
VMEM = pl.BlockSpec(memory_space=pltpu.VMEM)
SMEM = pl.BlockSpec(memory_space=pltpu.SMEM)


def dot(a, b, ca, cb):
    return lax.dot_general(a, b, (((ca,), (cb,)), ((), ())), preferred_element_type=F32)


def passed_along(array, axis, by):
    devices = lax.axis_size(axis)
    return lax.ppermute(array, axis, [(i, (i + by) % devices) for i in range(devices)])


def swapped(array, mask):
    devices = lax.axis_size("bond")
    return lax.ppermute(array, "bond", [(i, i ^ mask) for i in range(devices)])


def from_left(array, mask):
    slots, ranks = lax.axis_size("leaf"), lax.axis_size("bond")
    pairs = [
        (s * ranks + d, (s + 1) % slots * ranks + (d ^ mask)) for s in range(slots) for d in range(ranks)
    ]
    return lax.ppermute(array, ("leaf", "bond"), pairs)


def lookup(index_vector, charge_table, blocks):
    hits = index_vector[:, None] == blocks[None, :]
    return jnp.sum(jnp.where(hits, charge_table[None, :], 0), axis=1)


def shards_plain(isometries, leaf_ops, charges, assign):
    bond_rank = lax.axis_index("bond")
    weight = isometries[0]
    slab_rows = weight.shape[0]
    bond_width = weight.shape[1]
    op_count = leaf_ops.shape[1]
    charge_row = charges[0]
    blocks = jnp.arange(charge_row.shape[1], dtype=jnp.int32)
    left_index = (bond_rank * slab_rows + jnp.arange(slab_rows, dtype=jnp.int32)) // BLOCK
    full_index = jnp.arange(bond_width, dtype=jnp.int32) // BLOCK
    charge_left = lookup(left_index, charge_row[0], blocks)
    charge_right = lookup(full_index, charge_row[1], blocks)
    charge_parent = lookup(full_index, charge_row[2], blocks)
    charge_sum = (
        charge_left[:, None, None] + charge_right[None, :, None] - charge_parent[None, None, :]
    )
    keep_mask = jnp.mod(charge_sum, QMOD) == 0
    masked = jnp.where(keep_mask, weight, jnp.zeros((), weight.dtype))
    by_right = lax.all_to_all(masked, "bond", split_axis=1, concat_axis=0, tiled=True)
    take_left = (assign[0] != 1).astype(F32)
    take_right = (assign[0] != 0).astype(F32)
    held_ops = lax.all_gather(leaf_ops[0], "bond", axis=1, tiled=True)
    for level_now in range(1, LEVELS + 1):
        reach_by = 2 ** (level_now - 1)
        left_ops = passed_along(held_ops, "leaf", reach_by)
        left_mixed = jnp.dot(
            left_ops.reshape(op_count * bond_width, bond_width),
            by_right.reshape(bond_width, -1),
            preferred_element_type=F32,
        ).astype(BF16)
        left_mixed = left_mixed.reshape(op_count, -1, bond_width)
        left_part = jnp.einsum(
            "rp,krq->kpq",
            by_right.reshape(-1, bond_width),
            left_mixed,
            preferred_element_type=F32,
        )
        right_mixed = jnp.einsum(
            "kcb,abq->kacq", held_ops, masked, preferred_element_type=F32
        ).astype(BF16)
        right_part = jnp.einsum("acp,kacq->kpq", masked, right_mixed, preferred_element_type=F32)
        partial_sum = take_left[:, None, None] * left_part + take_right[:, None, None] * right_part
        held_ops = lax.psum(partial_sum, "bond").astype(BF16)
    result = lax.dynamic_slice_in_dim(held_ops, bond_rank * slab_rows, slab_rows, 1)
    return result[None]


CHARGES_AT = 2


class Info:
    def __init__(self, values, blocks):
        self.rank, self.assign = values[0], values[1]
        self.charge = lambda leg, block: values[CHARGES_AT + leg * blocks + block]
        self.blocks = blocks

    def fits(self, left, right, parent):
        total = self.charge(0, left) + self.charge(1, right) - self.charge(2, parent)
        return (total & (QMOD - 1)) == 0

    def ahead(self, left, right):
        count = jnp.int32(0)
        for k in range(self.blocks):
            for p in range(self.blocks):
                count += (self.fits(left, k, p) & (k < right)).astype(jnp.int32)
        return count


def add_group(op, mats, total):
    count, width = mats.shape[0], mats.shape[1]
    mixed = [dot(op, mats[j], 1, 0).astype(BF16) for j in range(count)]
    return total + dot(
        mats.reshape(count * width, width), jnp.concatenate(mixed, 0), 0, 0
    )


def pack_kernel(blocks, partners, masks, caps, charges, assign, *rest):
    weights, rest = rest[: len(masks)], rest[len(masks) :]
    branch, values, outs = rest[0], rest[1], rest[2:-4]
    stage, turned, turn, sems = rest[-4:]
    k = pl.program_id(0)

    @pl.when(k == 0)
    def _():
        values[0] = lax.axis_index("bond")
        values[1] = assign[0, 0]
        for leg in range(3):
            for block in range(blocks):
                values[CHARGES_AT + leg * blocks + block] = charges[0, leg, block]

    info = Info(values, blocks)
    rank = info.rank
    area = GROUP * ROWS
    slab, width = weights[0].shape[0], weights[0].shape[-1]
    quarters = slab // GROUP

    @pl.when(k == 0)
    def _():
        to = lax.broadcasted_iota(jnp.int32, (area, area), 0)
        at = lax.broadcasted_iota(jnp.int32, (area, area), 1)
        turn[...] = jnp.where(at == (to % GROUP) * ROWS + to // GROUP, 1.0, 0.0).astype(BF16)
        need = lax.fori_loop(
            0,
            blocks,
            lambda d, most: jnp.maximum(most, info.ahead(d, blocks)),
            jnp.int32(0),
        )
        step = jnp.int32(1)
        for cap in caps[:-1]:
            step += (need > cap).astype(jnp.int32)
        branch[0] = jnp.where(info.assign == 1, 0, step)

    allowed = [info.fits(rank, k, p) for p in range(blocks)]
    some = functools.reduce(jnp.logical_or, allowed)

    @pl.when(some & (info.assign != 1))
    def _():
        for n in range(len(masks)):
            for g in range(quarters):
                rows = weights[n][g * GROUP : (g + 1) * GROUP].reshape(area, width)
                turned[n, g] = dot(turn[...], rows, 1, 0).astype(BF16)
        slot = info.ahead(rank, k)
        for p in range(blocks):

            @pl.when(allowed[p])
            def _():
                lanes = slice(p * BLOCK, (p + 1) * BLOCK)
                for n in range(len(masks)):
                    for h in range(quarters // 2):
                        both = jnp.concatenate(
                            [turned[n, h, :, lanes], turned[n, h + quarters // 2, :, lanes]], axis=1
                        )
                        stage[n, slot, :, h * GROUP : (h + 1) * GROUP, :] = both.reshape(
                            ROWS, GROUP, 2 * BLOCK
                        )

            slot = slot + allowed[p].astype(jnp.int32)

    def leave(g, cap):
        copies = [
            pltpu.make_async_copy(
                stage.at[n, pl.ds(0, cap)], outs[g * len(masks) + n], sems.at[n]
            )
            for n in range(len(masks))
        ]
        for copy in copies:
            copy.start()
        for copy in copies:
            copy.wait()

    @pl.when(k == blocks - 1)
    def _():
        for g, cap in enumerate(caps):
            pl.when(branch[0] == g + 1)(functools.partial(leave, g, cap))


def pack(charges, assign, weight, masks, caps):
    slab, width = weight.shape[0], weight.shape[1]
    partners = lax.axis_size("bond")
    blocks = width // BLOCK
    cut = weight.reshape(slab, blocks, partners, ROWS, width)
    piece = (ROWS, slab // 2, 2 * BLOCK)

    def rows_for(m):
        return pl.BlockSpec(
            (slab, None, None, ROWS, width),
            lambda k, *_: (0, k, lax.axis_index("bond") ^ m, 0, 0),
        )

    branch, info, *arrays = pl.pallas_call(
        functools.partial(pack_kernel, blocks, partners, masks, caps),
        grid=(blocks,),
        in_specs=[SMEM, SMEM] + [rows_for(m) for m in masks],
        out_specs=[SMEM, SMEM] + [ANY] * (len(caps) * len(masks)),
        out_shape=[
            jax.ShapeDtypeStruct((1,), jnp.int32),
            jax.ShapeDtypeStruct((CHARGES_AT + 3 * blocks,), jnp.int32),
        ]
        + [jax.ShapeDtypeStruct((cap,) + piece, BF16) for cap in caps for _ in masks],
        scratch_shapes=[
            pltpu.VMEM((len(masks), blocks * blocks) + piece, BF16),
            pltpu.VMEM((len(masks), slab // GROUP, GROUP * ROWS, width), BF16),
            pltpu.VMEM((GROUP * ROWS, GROUP * ROWS), BF16),
            pltpu.SemaphoreType.DMA((len(masks),)),
        ],
        compiler_params=pltpu.CompilerParams(vmem_limit_bytes=24 * MIB),
        name="pack",
    )(charges, assign, *[cut] * len(masks))
    each = len(masks)
    return branch[0], info, [arrays[g * each : (g + 1) * each] for g in range(len(caps))]


def first_left_kernel(partners, per, values, before, own, *rest):
    come, ops = rest[: partners - 1], rest[partners - 1 : -5]
    out, after, mats, op, sems = rest[-5:]
    width = mats.shape[-1]
    blocks = width // BLOCK
    info = Info(values, blocks)
    each, half = own.shape[1:3]
    low = lax.broadcasted_iota(jnp.int32, (each, half, 2 * BLOCK), 2) < BLOCK

    def leave(k):
        rows = pl.ds(pl.multiple_of(k * each, each), each)
        return pltpu.make_async_copy(mats.at[rows], out.at[rows], sems.at[k])

    def step(k, slots):
        rows = pl.ds(pl.multiple_of(k * each, each), each)
        after = []
        for m in range(partners):
            source = info.rank ^ m
            pieces = come[m - 1] if m else own
            last = pieces.shape[0] - 1
            slot = slots[m]
            for tile in range(blocks // 2):
                first = info.fits(source, k, 2 * tile)
                second = info.fits(source, k, 2 * tile + 1)
                middle = slot + first.astype(jnp.int32)
                at = pl.multiple_of(source * 2 * half, half)
                lanes = slice(tile * 2 * BLOCK, (tile + 1) * 2 * BLOCK)

                a = pieces[jnp.minimum(slot, last)]
                b = pieces[jnp.minimum(middle, last)]
                keep = jnp.where(low, first.astype(jnp.int32), second.astype(jnp.int32)) != 0
                upper = jnp.concatenate([a[..., :BLOCK], b[..., :BLOCK]], axis=-1)
                mats[rows, pl.ds(at, half), lanes] = jnp.where(keep, upper, 0)
                lower = jnp.concatenate([a[..., BLOCK:], b[..., BLOCK:]], axis=-1)
                mats[rows, pl.ds(at + half, half), lanes] = jnp.where(keep, lower, 0)
                slot = middle + second.astype(jnp.int32)
            after.append(slot)
        leave(k).start()
        return tuple(after)

    lax.fori_loop(0, blocks, step, (jnp.int32(0),) * partners)
    rows = ops[0].shape[0]
    for m in range(partners):
        op[pl.ds(pl.multiple_of((info.rank ^ m) * rows, rows), rows)] = ops[m][...]
    after[...] = before[...]

    @pl.loop(0, mats.shape[0] // per)
    def _(c):
        group = mats[pl.ds(pl.multiple_of(c * per, per), per)]
        after[...] = add_group(op[...], group, after[...])

    @pl.loop(0, blocks)
    def _(k):
        leave(k).wait()


def first_left(info, op, before, own, come, per):
    width = before.shape[-1]
    blocks = width // BLOCK
    whole = (own.shape[1] * blocks, width, width)
    return pl.pallas_call(
        functools.partial(first_left_kernel, len(come) + 1, per),
        in_specs=[SMEM, VMEM, VMEM] + [VMEM] * (len(come) + len(op)),
        out_specs=[ANY, VMEM],
        out_shape=[jax.ShapeDtypeStruct(whole, BF16), jax.ShapeDtypeStruct((width, width), F32)],
        scratch_shapes=[
            pltpu.VMEM(whole, BF16),
            pltpu.VMEM((width, width), BF16),
            pltpu.SemaphoreType.DMA((blocks,)),
        ],
        compiler_params=pltpu.CompilerParams(vmem_limit_bytes=32 * MIB),
        name="first_left",
    )(info, before, own, *come, *op)


def unset(shape):
    return pl.pallas_call(
        lambda out: None,
        out_specs=ANY,
        out_shape=jax.ShapeDtypeStruct(shape, BF16),
        name="unset",
    )()


def mask_of(info, width):
    blocks = width // BLOCK

    def spread(shape, axis, leg):
        block = lax.broadcasted_iota(jnp.int32, shape, axis) // BLOCK
        charge = jnp.zeros(shape, jnp.int32)
        for k in range(blocks):
            charge = jnp.where(block == k, info.charge(leg, k), charge)
        return charge

    left = info.charge(0, info.rank)
    total = left + spread((width, width), 0, 1) - spread((width, width), 1, 2)
    return jnp.where((total & (QMOD - 1)) == 0, 1.0, 0.0).astype(BF16)


def side_kernel(not_if, masked, per, quarters, values, before, mats, *rest):
    ops, (after, held, whole, sems, op_sems) = rest[:quarters], rest[quarters:]
    info = Info(values, mats.shape[-1] // BLOCK)
    after[...] = before[...]
    rows = ops[0].shape[0]
    count = mats.shape[0] // per
    ahead = min(count, 4) if per < 16 else 1

    def load(c):
        part = pl.ds(c * per, per)
        return pltpu.make_async_copy(mats.at[part], held.at[c], sems.at[c])

    @pl.when(info.assign != not_if)
    def _():
        for c in range(ahead):
            load(c).start()
        moves = []
        for m in range(quarters if quarters > 1 else 0):
            to = whole.at[pl.ds(pl.multiple_of((info.rank ^ m) * rows, rows), rows)]
            moves.append(pltpu.make_async_copy(ops[m], to, op_sems.at[m]))
        for move in moves:
            move.start()
        mask = mask_of(info, whole.shape[0]) if masked else None
        for move in moves:
            move.wait()
        op = whole if quarters > 1 else ops[0]

        @pl.loop(0, count)
        def _(c):
            pl.when(c + ahead < count)(lambda: load(c + ahead).start())
            load(c).wait()
            group = held[c]
            if masked:
                group = group * mask[None]
            after[...] = add_group(op[...], group, after[...])


def side(not_if, info, op, before, mats, masked, per):
    total, width = mats.shape[0], mats.shape[-1]
    ops = op if isinstance(op, (list, tuple)) else [op]
    return pl.pallas_call(
        functools.partial(side_kernel, not_if, masked, per, len(ops)),
        in_specs=[SMEM, VMEM, ANY] + [ANY if len(ops) > 1 else VMEM] * len(ops),
        out_specs=VMEM,
        out_shape=jax.ShapeDtypeStruct((width, width), F32),
        scratch_shapes=[
            pltpu.VMEM((total // per, per, width, width), BF16),
            pltpu.VMEM((width, width), BF16),
            pltpu.SemaphoreType.DMA((total // per,)),
            pltpu.SemaphoreType.DMA((len(ops),)),
        ],
        compiler_params=pltpu.CompilerParams(vmem_limit_bytes=28 * MIB),
        cost_estimate=pl.CostEstimate(
            flops=4 * total * width**3, bytes_accessed=2 * total * width**2, transcendentals=0
        ),
        name="side",
    )(info, before, mats, *ops)


def shards(isometries, leaf_ops, charges, assign):
    rank = lax.axis_index("bond")
    partners = lax.axis_size("bond")
    weight = isometries[0]
    slab, width = weight.shape[0], weight.shape[1]
    own = leaf_ops[0, 0]
    zeros = jnp.zeros((width, width), F32)
    share = (ROWS * (width // BLOCK), width, width)
    small, large = 4, 32

    def gathered(part):
        return [part] + [swapped(part, m) for m in range(1, partners)]

    op = gathered(own)
    left = [from_left(own, m) for m in (0, partners - 1)]
    branch, info, packed = pack(charges, assign, weight, range(partners), CAPACITIES)

    def without(info, weight, op, left, packed):
        return side(0, info, op, zeros, weight, True, small), unset(share)

    def exchange(g, info, weight, op, left, packed):
        mine, *sent = packed[g]
        come = [swapped(part, m + 1) for m, part in enumerate(sent)]
        total = side(0, info, op, zeros, weight, True, small)
        *left, total = lax.optimization_barrier((*left, total))
        left_op = [left[0]] + [swapped(left[0], m) for m in range(1, partners - 1)] + [left[1]]
        mats, total = first_left(info, left_op, total, mine, come, 16)
        return total, mats

    total, mats = lax.switch(
        branch,
        [without] + [functools.partial(exchange, g) for g in range(len(CAPACITIES))],
        info, weight, op, left, packed,
    )
    for level in range(2, LEVELS + 1):
        sent = total.astype(BF16)
        come = [swapped(sent, m) for m in range(1, partners)]
        op = (total + sum(c.astype(F32) for c in come)).astype(BF16)
        left_op = passed_along(op, "leaf", 2 ** (level - 1))
        total = side(0, info, op, zeros, weight, True, 32)
        total = side(1, info, left_op, total, mats, False, large)

    def rows_of(m):
        return lax.dynamic_slice_in_dim(total, (rank ^ m) * slab, slab, 0)

    result = rows_of(0)
    for m in range(1, partners):
        result = result + swapped(rows_of(m).astype(BF16), m).astype(F32)
    return result.astype(BF16)[None, None]


def solution(mesh):
    in_specs = (
        P("leaf", "bond", None, None),
        P("leaf", None, "bond", None),
        P("leaf", None, None),
        P("leaf", None),
    )
    out_specs = P("leaf", None, "bond", None)
    partners = mesh.shape["bond"]

    def whole(isometries, leaf_ops, charges, assign):
        width = isometries.shape[1]
        fits = (
            partners & (partners - 1) == 0
            and width // partners == BLOCK
            and BLOCK == partners * ROWS
            and charges.shape[2] * BLOCK == width
            and leaf_ops.shape[1] == 1
        )
        return jax.shard_map(
            shards if fits else shards_plain,
            mesh=mesh, in_specs=in_specs, out_specs=out_specs, check_vma=False,
        )(isometries, leaf_ops, charges, assign)

    return whole
```

```python
import functools

import jax
import jax.numpy as jnp
from jax import lax
from jax.experimental import pallas as pl
from jax.experimental.pallas import tpu as pltpu
from jax.sharding import PartitionSpec as P

BLOCK = 64
QMOD = 4
LEVELS = 3
ROWS = 16
GROUP = 16
CAPACITIES = (5, 6, 7, 8, 10, 16)
F32 = jnp.float32
BF16 = jnp.bfloat16
MIB = 2**20
ANY = pl.BlockSpec(memory_space=pl.ANY)
VMEM = pl.BlockSpec(memory_space=pltpu.VMEM)
SMEM = pl.BlockSpec(memory_space=pltpu.SMEM)


def dot(a, b, ca, cb):
    return lax.dot_general(a, b, (((ca,), (cb,)), ((), ())), preferred_element_type=F32)


def passed_along(array, axis, by):
    devices = lax.axis_size(axis)
    return lax.ppermute(array, axis, [(i, (i + by) % devices) for i in range(devices)])


def swapped(array, mask):
    devices = lax.axis_size("bond")
    return lax.ppermute(array, "bond", [(i, i ^ mask) for i in range(devices)])


def from_left(array, mask):
    slots, ranks = lax.axis_size("leaf"), lax.axis_size("bond")
    pairs = [
        (s * ranks + d, (s + 1) % slots * ranks + (d ^ mask)) for s in range(slots) for d in range(ranks)
    ]
    return lax.ppermute(array, ("leaf", "bond"), pairs)


def lookup(index_vector, charge_table, blocks):
    hits = index_vector[:, None] == blocks[None, :]
    return jnp.sum(jnp.where(hits, charge_table[None, :], 0), axis=1)


def shards_plain(isometries, leaf_ops, charges, assign):
    bond_rank = lax.axis_index("bond")
    weight = isometries[0]
    slab_rows = weight.shape[0]
    bond_width = weight.shape[1]
    op_count = leaf_ops.shape[1]
    charge_row = charges[0]
    blocks = jnp.arange(charge_row.shape[1], dtype=jnp.int32)
    left_index = (bond_rank * slab_rows + jnp.arange(slab_rows, dtype=jnp.int32)) // BLOCK
    full_index = jnp.arange(bond_width, dtype=jnp.int32) // BLOCK
    charge_left = lookup(left_index, charge_row[0], blocks)
    charge_right = lookup(full_index, charge_row[1], blocks)
    charge_parent = lookup(full_index, charge_row[2], blocks)
    charge_sum = (
        charge_left[:, None, None] + charge_right[None, :, None] - charge_parent[None, None, :]
    )
    keep_mask = jnp.mod(charge_sum, QMOD) == 0
    masked = jnp.where(keep_mask, weight, jnp.zeros((), weight.dtype))
    by_right = lax.all_to_all(masked, "bond", split_axis=1, concat_axis=0, tiled=True)
    take_left = (assign[0] != 1).astype(F32)
    take_right = (assign[0] != 0).astype(F32)
    held_ops = lax.all_gather(leaf_ops[0], "bond", axis=1, tiled=True)
    for level_now in range(1, LEVELS + 1):
        reach_by = 2 ** (level_now - 1)
        left_ops = passed_along(held_ops, "leaf", reach_by)
        left_mixed = jnp.dot(
            left_ops.reshape(op_count * bond_width, bond_width),
            by_right.reshape(bond_width, -1),
            preferred_element_type=F32,
        ).astype(BF16)
        left_mixed = left_mixed.reshape(op_count, -1, bond_width)
        left_part = jnp.einsum(
            "rp,krq->kpq",
            by_right.reshape(-1, bond_width),
            left_mixed,
            preferred_element_type=F32,
        )
        right_mixed = jnp.einsum(
            "kcb,abq->kacq", held_ops, masked, preferred_element_type=F32
        ).astype(BF16)
        right_part = jnp.einsum("acp,kacq->kpq", masked, right_mixed, preferred_element_type=F32)
        partial_sum = take_left[:, None, None] * left_part + take_right[:, None, None] * right_part
        held_ops = lax.psum(partial_sum, "bond").astype(BF16)
    result = lax.dynamic_slice_in_dim(held_ops, bond_rank * slab_rows, slab_rows, 1)
    return result[None]


CHARGES_AT = 2


class Info:
    def __init__(self, values, blocks):
        self.rank, self.assign = values[0], values[1]
        self.charge = lambda leg, block: values[CHARGES_AT + leg * blocks + block]
        self.blocks = blocks

    def fits(self, left, right, parent):
        total = self.charge(0, left) + self.charge(1, right) - self.charge(2, parent)
        return (total & (QMOD - 1)) == 0

    def ahead(self, left, right):
        count = jnp.int32(0)
        for k in range(self.blocks):
            for p in range(self.blocks):
                count += (self.fits(left, k, p) & (k < right)).astype(jnp.int32)
        return count


def add_group(op, mats, total):
    count, width = mats.shape[0], mats.shape[1]
    mixed = [dot(op, mats[j], 1, 0).astype(BF16) for j in range(count)]
    return total + dot(
        mats.reshape(count * width, width), jnp.concatenate(mixed, 0), 0, 0
    )


def pack_kernel(blocks, partners, masks, caps, charges, assign, *rest):
    weights, rest = rest[: len(masks)], rest[len(masks) :]
    branch, values, outs = rest[0], rest[1], rest[2:-4]
    stage, turned, turn, sems = rest[-4:]
    k = pl.program_id(0)

    @pl.when(k == 0)
    def _():
        values[0] = lax.axis_index("bond")
        values[1] = assign[0, 0]
        for leg in range(3):
            for block in range(blocks):
                values[CHARGES_AT + leg * blocks + block] = charges[leg, 0, block]

    info = Info(values, blocks)
    rank = info.rank
    area = GROUP * ROWS
    slab, width = weights[0].shape[0], weights[0].shape[-1]
    quarters = slab // GROUP

    @pl.when(k == 0)
    def _():
        to = lax.broadcasted_iota(jnp.int32, (area, area), 0)
        at = lax.broadcasted_iota(jnp.int32, (area, area), 1)
        turn[...] = jnp.where(at == (to % GROUP) * ROWS + to // GROUP, 1.0, 0.0).astype(BF16)
        need = lax.fori_loop(
            0,
            blocks,
            lambda d, most: jnp.maximum(most, info.ahead(d, blocks)),
            jnp.int32(0),
        )
        step = jnp.int32(1)
        for cap in caps[:-1]:
            step += (need > cap).astype(jnp.int32)
        branch[0] = jnp.where(info.assign == 1, 0, step)

    allowed = [info.fits(rank, k, p) for p in range(blocks)]
    some = functools.reduce(jnp.logical_or, allowed)

    @pl.when(some & (info.assign != 1))
    def _():
        for n in range(len(masks)):
            for g in range(quarters):
                rows = weights[n][g * GROUP : (g + 1) * GROUP].reshape(area, width)
                turned[n, g] = dot(turn[...], rows, 1, 0).astype(BF16)
        slot = info.ahead(rank, k)
        for p in range(blocks):

            @pl.when(allowed[p])
            def _():
                lanes = slice(p * BLOCK, (p + 1) * BLOCK)
                for n in range(len(masks)):
                    for h in range(quarters // 2):
                        both = jnp.concatenate(
                            [turned[n, h, :, lanes], turned[n, h + quarters // 2, :, lanes]], axis=1
                        )
                        stage[n, slot, :, h * GROUP : (h + 1) * GROUP, :] = both.reshape(
                            ROWS, GROUP, 2 * BLOCK
                        )

            slot = slot + allowed[p].astype(jnp.int32)

    def leave(g, cap):
        copies = [
            pltpu.make_async_copy(
                stage.at[n, pl.ds(0, cap)], outs[g * len(masks) + n], sems.at[n]
            )
            for n in range(len(masks))
        ]
        for copy in copies:
            copy.start()
        for copy in copies:
            copy.wait()

    @pl.when(k == blocks - 1)
    def _():
        for g, cap in enumerate(caps):
            pl.when(branch[0] == g + 1)(functools.partial(leave, g, cap))


def pack(charges, assign, weight, masks, caps):
    slab, width = weight.shape[0], weight.shape[1]
    partners = lax.axis_size("bond")
    blocks = width // BLOCK
    cut = weight.reshape(slab, blocks, partners, ROWS, width)
    piece = (ROWS, slab // 2, 2 * BLOCK)

    def rows_for(m):
        return pl.BlockSpec(
            (slab, None, None, ROWS, width),
            lambda k, *_: (0, k, lax.axis_index("bond") ^ m, 0, 0),
        )

    branch, info, *arrays = pl.pallas_call(
        functools.partial(pack_kernel, blocks, partners, masks, caps),
        grid=(blocks,),
        in_specs=[SMEM, SMEM] + [rows_for(m) for m in masks],
        out_specs=[SMEM, SMEM] + [ANY] * (len(caps) * len(masks)),
        out_shape=[
            jax.ShapeDtypeStruct((1,), jnp.int32),
            jax.ShapeDtypeStruct((CHARGES_AT + 3 * blocks,), jnp.int32),
        ]
        + [jax.ShapeDtypeStruct((cap,) + piece, BF16) for cap in caps for _ in masks],
        scratch_shapes=[
            pltpu.VMEM((len(masks), blocks * blocks) + piece, BF16),
            pltpu.VMEM((len(masks), slab // GROUP, GROUP * ROWS, width), BF16),
            pltpu.VMEM((GROUP * ROWS, GROUP * ROWS), BF16),
            pltpu.SemaphoreType.DMA((len(masks),)),
        ],
        compiler_params=pltpu.CompilerParams(vmem_limit_bytes=24 * MIB),
        name="pack",
    )(jnp.swapaxes(charges, 0, 1), assign, *[cut] * len(masks))
    each = len(masks)
    return branch[0], info, [arrays[g * each : (g + 1) * each] for g in range(len(caps))]


def first_left_kernel(partners, per, values, before, own, *rest):
    come, ops = rest[: partners - 1], rest[partners - 1 : -6]
    out, sent, mats, op, after, sems = rest[-6:]
    width = mats.shape[-1]
    blocks = width // BLOCK
    info = Info(values, blocks)
    each, half = own.shape[1:3]
    low = lax.broadcasted_iota(jnp.int32, (each, half, 2 * BLOCK), 2) < BLOCK

    def leave(k):
        rows = pl.ds(pl.multiple_of(k * each, each), each)
        return pltpu.make_async_copy(mats.at[rows], out.at[rows], sems.at[k])

    def step(k, slots):
        rows = pl.ds(pl.multiple_of(k * each, each), each)
        after = []
        for m in range(partners):
            source = info.rank ^ m
            pieces = come[m - 1] if m else own
            last = pieces.shape[0] - 1
            slot = slots[m]
            for tile in range(blocks // 2):
                first = info.fits(source, k, 2 * tile)
                second = info.fits(source, k, 2 * tile + 1)
                middle = slot + first.astype(jnp.int32)
                at = pl.multiple_of(source * 2 * half, half)
                lanes = slice(tile * 2 * BLOCK, (tile + 1) * 2 * BLOCK)

                a = pieces[jnp.minimum(slot, last)]
                b = pieces[jnp.minimum(middle, last)]
                keep = jnp.where(low, first.astype(jnp.int32), second.astype(jnp.int32)) != 0
                upper = jnp.concatenate([a[..., :BLOCK], b[..., :BLOCK]], axis=-1)
                mats[rows, pl.ds(at, half), lanes] = jnp.where(keep, upper, 0)
                lower = jnp.concatenate([a[..., BLOCK:], b[..., BLOCK:]], axis=-1)
                mats[rows, pl.ds(at + half, half), lanes] = jnp.where(keep, lower, 0)
                slot = middle + second.astype(jnp.int32)
            after.append(slot)
        leave(k).start()
        return tuple(after)

    lax.fori_loop(0, blocks, step, (jnp.int32(0),) * partners)
    rows = ops[0].shape[0]
    for m in range(partners):
        op[pl.ds(pl.multiple_of((info.rank ^ m) * rows, rows), rows)] = ops[m][...]
    after[...] = before[...]

    @pl.loop(0, mats.shape[0] // per)
    def _(c):
        group = mats[pl.ds(pl.multiple_of(c * per, per), per)]
        after[...] = add_group(op[...], group, after[...])

    sent[...] = after[...].astype(BF16)

    @pl.loop(0, blocks)
    def _(k):
        leave(k).wait()


def first_left(info, op, before, own, come, per):
    width = before.shape[-1]
    blocks = width // BLOCK
    whole = (own.shape[1] * blocks, width, width)
    return pl.pallas_call(
        functools.partial(first_left_kernel, len(come) + 1, per),
        in_specs=[SMEM, VMEM, VMEM] + [VMEM] * (len(come) + len(op)),
        out_specs=[ANY, VMEM],
        out_shape=[jax.ShapeDtypeStruct(whole, BF16), jax.ShapeDtypeStruct((width, width), BF16)],
        scratch_shapes=[
            pltpu.VMEM(whole, BF16),
            pltpu.VMEM((width, width), BF16),
            pltpu.VMEM((width, width), F32),
            pltpu.SemaphoreType.DMA((blocks,)),
        ],
        compiler_params=pltpu.CompilerParams(vmem_limit_bytes=32 * MIB),
        name="first_left",
    )(info, before, own, *come, *op)


def unset(shape):
    return pl.pallas_call(
        lambda out: None,
        out_specs=ANY,
        out_shape=jax.ShapeDtypeStruct(shape, BF16),
        name="unset",
    )()


def mask_of(info, width):
    blocks = width // BLOCK

    def spread(shape, axis, leg):
        block = lax.broadcasted_iota(jnp.int32, shape, axis) // BLOCK
        charge = jnp.zeros(shape, jnp.int32)
        for k in range(blocks):
            charge = jnp.where(block == k, info.charge(leg, k), charge)
        return charge

    left = info.charge(0, info.rank)
    total = left + spread((width, width), 0, 1) - spread((width, width), 1, 2)
    return jnp.where((total & (QMOD - 1)) == 0, 1.0, 0.0).astype(BF16)


def side_kernel(not_if, masked, per, quarters, values, before, mats, *rest):
    ops, (out, held, whole, after, sems, op_sems) = rest[:quarters], rest[quarters:]
    info = Info(values, mats.shape[-1] // BLOCK)
    after[...] = before[...]
    rows = ops[0].shape[0]
    count = mats.shape[0] // per
    ahead = min(count, 4) if per < 16 else 1

    def load(c):
        part = pl.ds(c * per, per)
        return pltpu.make_async_copy(mats.at[part], held.at[c], sems.at[c])

    @pl.when(info.assign != not_if)
    def _():
        for c in range(ahead):
            load(c).start()
        moves = []
        for m in range(quarters if quarters > 1 else 0):
            to = whole.at[pl.ds(pl.multiple_of((info.rank ^ m) * rows, rows), rows)]
            moves.append(pltpu.make_async_copy(ops[m], to, op_sems.at[m]))
        for move in moves:
            move.start()
        mask = mask_of(info, whole.shape[0]) if masked else None
        for move in moves:
            move.wait()
        op = whole if quarters > 1 else ops[0]

        @pl.loop(0, count)
        def _(c):
            pl.when(c + ahead < count)(lambda: load(c + ahead).start())
            load(c).wait()
            group = held[c]
            if masked:
                group = group * mask[None]
            after[...] = add_group(op[...], group, after[...])

    out[...] = after[...].astype(out.dtype)


def side(not_if, info, op, before, mats, masked, per, kind=F32):
    total, width = mats.shape[0], mats.shape[-1]
    ops = op if isinstance(op, (list, tuple)) else [op]
    return pl.pallas_call(
        functools.partial(side_kernel, not_if, masked, per, len(ops)),
        in_specs=[SMEM, VMEM, ANY] + [ANY if len(ops) > 1 else VMEM] * len(ops),
        out_specs=VMEM,
        out_shape=jax.ShapeDtypeStruct((width, width), kind),
        scratch_shapes=[
            pltpu.VMEM((total // per, per, width, width), BF16),
            pltpu.VMEM((width, width), BF16),
            pltpu.VMEM((width, width), F32),
            pltpu.SemaphoreType.DMA((total // per,)),
            pltpu.SemaphoreType.DMA((len(ops),)),
        ],
        compiler_params=pltpu.CompilerParams(vmem_limit_bytes=28 * MIB),
        cost_estimate=pl.CostEstimate(
            flops=4 * total * width**3, bytes_accessed=2 * total * width**2, transcendentals=0
        ),
        name="side",
    )(info, before, mats, *ops)


def shards(isometries, leaf_ops, charges, assign):
    rank = lax.axis_index("bond")
    partners = lax.axis_size("bond")
    weight = isometries[0]
    slab, width = weight.shape[0], weight.shape[1]
    own = leaf_ops[0, 0]
    zeros = jnp.zeros((width, width), F32)
    share = (ROWS * (width // BLOCK), width, width)
    small, large = 4, 32

    def gathered(part):
        return [part] + [swapped(part, m) for m in range(1, partners)]

    op = gathered(own)
    left = [from_left(own, m) for m in (0, partners - 1)]
    branch, info, packed = pack(charges, assign, weight, range(partners), CAPACITIES)

    def without(info, weight, op, left, packed):
        return side(0, info, op, zeros, weight, True, small, BF16), unset(share)

    def exchange(g, info, weight, op, left, packed):
        mine, *others = packed[g]
        come = [swapped(part, m + 1) for m, part in enumerate(others)]
        total = side(0, info, op, zeros, weight, True, small)
        *left, total = lax.optimization_barrier((*left, total))
        left_op = [left[0]] + [swapped(left[0], m) for m in range(1, partners - 1)] + [left[1]]
        mats, sent = first_left(info, left_op, total, mine, come, 16)
        return sent, mats

    sent, mats = lax.switch(
        branch,
        [without] + [functools.partial(exchange, g) for g in range(len(CAPACITIES))],
        info, weight, op, left, packed,
    )
    for level in range(2, LEVELS + 1):
        come = [swapped(sent, m) for m in range(1, partners)]
        op = sum(c.astype(F32) for c in [sent] + come).astype(BF16)
        left_op = passed_along(op, "leaf", 2 ** (level - 1))
        total = side(0, info, op, zeros, weight, True, 32)
        sent = side(1, info, left_op, total, mats, False, large, BF16)

    def rows_of(m):
        return lax.dynamic_slice_in_dim(sent, (rank ^ m) * slab, slab, 0)

    result = rows_of(0).astype(F32)
    for m in range(1, partners):
        result = result + swapped(rows_of(m), m).astype(F32)
    return result.astype(BF16)[None, None]


def solution(mesh):
    in_specs = (
        P("leaf", "bond", None, None),
        P("leaf", None, "bond", None),
        P("leaf", None, None),
        P("leaf", None),
    )
    out_specs = P("leaf", None, "bond", None)
    partners = mesh.shape["bond"]

    def whole(isometries, leaf_ops, charges, assign):
        width = isometries.shape[1]
        fits = (
            partners & (partners - 1) == 0
            and width // partners == BLOCK
            and BLOCK == partners * ROWS
            and charges.shape[2] * BLOCK == width
            and leaf_ops.shape[1] == 1
        )
        return jax.shard_map(
            shards if fits else shards_plain,
            mesh=mesh, in_specs=in_specs, out_specs=out_specs, check_vma=False,
        )(isometries, leaf_ops, charges, assign)

    return whole
```

```python
import functools

import jax
import jax.numpy as jnp
from jax import lax
from jax.experimental import pallas as pl
from jax.experimental.pallas import tpu as pltpu
from jax.sharding import PartitionSpec as P

BLOCK = 64
QMOD = 4
LEVELS = 3
ROWS = 16
GROUP = 16
CAPACITIES = (5, 6, 7, 8, 10, 16)
F32 = jnp.float32
BF16 = jnp.bfloat16
MIB = 2**20
ANY = pl.BlockSpec(memory_space=pl.ANY)
VMEM = pl.BlockSpec(memory_space=pltpu.VMEM)
SMEM = pl.BlockSpec(memory_space=pltpu.SMEM)


def dot(a, b, ca, cb):
    return lax.dot_general(a, b, (((ca,), (cb,)), ((), ())), preferred_element_type=F32)


def passed_along(array, axis, by):
    devices = lax.axis_size(axis)
    return lax.ppermute(array, axis, [(i, (i + by) % devices) for i in range(devices)])


def swapped(array, mask):
    devices = lax.axis_size("bond")
    return lax.ppermute(array, "bond", [(i, i ^ mask) for i in range(devices)])


def from_left(array, mask):
    slots, ranks = lax.axis_size("leaf"), lax.axis_size("bond")
    pairs = [
        (s * ranks + d, (s + 1) % slots * ranks + (d ^ mask)) for s in range(slots) for d in range(ranks)
    ]
    return lax.ppermute(array, ("leaf", "bond"), pairs)


def lookup(index_vector, charge_table, blocks):
    hits = index_vector[:, None] == blocks[None, :]
    return jnp.sum(jnp.where(hits, charge_table[None, :], 0), axis=1)


def shards_plain(isometries, leaf_ops, charges, assign):
    bond_rank = lax.axis_index("bond")
    weight = isometries[0]
    slab_rows = weight.shape[0]
    bond_width = weight.shape[1]
    op_count = leaf_ops.shape[1]
    charge_row = charges[0]
    blocks = jnp.arange(charge_row.shape[1], dtype=jnp.int32)
    left_index = (bond_rank * slab_rows + jnp.arange(slab_rows, dtype=jnp.int32)) // BLOCK
    full_index = jnp.arange(bond_width, dtype=jnp.int32) // BLOCK
    charge_left = lookup(left_index, charge_row[0], blocks)
    charge_right = lookup(full_index, charge_row[1], blocks)
    charge_parent = lookup(full_index, charge_row[2], blocks)
    charge_sum = (
        charge_left[:, None, None] + charge_right[None, :, None] - charge_parent[None, None, :]
    )
    keep_mask = jnp.mod(charge_sum, QMOD) == 0
    masked = jnp.where(keep_mask, weight, jnp.zeros((), weight.dtype))
    by_right = lax.all_to_all(masked, "bond", split_axis=1, concat_axis=0, tiled=True)
    take_left = (assign[0] != 1).astype(F32)
    take_right = (assign[0] != 0).astype(F32)
    held_ops = lax.all_gather(leaf_ops[0], "bond", axis=1, tiled=True)
    for level_now in range(1, LEVELS + 1):
        reach_by = 2 ** (level_now - 1)
        left_ops = passed_along(held_ops, "leaf", reach_by)
        left_mixed = jnp.dot(
            left_ops.reshape(op_count * bond_width, bond_width),
            by_right.reshape(bond_width, -1),
            preferred_element_type=F32,
        ).astype(BF16)
        left_mixed = left_mixed.reshape(op_count, -1, bond_width)
        left_part = jnp.einsum(
            "rp,krq->kpq",
            by_right.reshape(-1, bond_width),
            left_mixed,
            preferred_element_type=F32,
        )
        right_mixed = jnp.einsum(
            "kcb,abq->kacq", held_ops, masked, preferred_element_type=F32
        ).astype(BF16)
        right_part = jnp.einsum("acp,kacq->kpq", masked, right_mixed, preferred_element_type=F32)
        partial_sum = take_left[:, None, None] * left_part + take_right[:, None, None] * right_part
        held_ops = lax.psum(partial_sum, "bond").astype(BF16)
    result = lax.dynamic_slice_in_dim(held_ops, bond_rank * slab_rows, slab_rows, 1)
    return result[None]


CHARGES_AT = 2


class Info:
    def __init__(self, values, blocks):
        self.rank, self.assign = values[0], values[1]
        self.charge = lambda leg, block: values[CHARGES_AT + leg * blocks + block]
        self.blocks = blocks

    def fits(self, left, right, parent):
        total = self.charge(0, left) + self.charge(1, right) - self.charge(2, parent)
        return (total & (QMOD - 1)) == 0

    def ahead(self, left, right):
        count = jnp.int32(0)
        for k in range(self.blocks):
            for p in range(self.blocks):
                count += (self.fits(left, k, p) & (k < right)).astype(jnp.int32)
        return count


def add_group(op, mats, total):
    count, width = mats.shape[0], mats.shape[1]
    mixed = [dot(op, mats[j], 1, 0).astype(BF16) for j in range(count)]
    return total + dot(
        mats.reshape(count * width, width), jnp.concatenate(mixed, 0), 0, 0
    )


def pack_kernel(blocks, partners, masks, caps, charges, assign, *rest):
    weights, rest = rest[: len(masks)], rest[len(masks) :]
    branch, values, outs = rest[0], rest[1], rest[2:-4]
    stage, turned, turn, sems = rest[-4:]
    k = pl.program_id(0)

    @pl.when(k == 0)
    def _():
        values[0] = lax.axis_index("bond")
        values[1] = assign[0, 0]
        for leg in range(3):
            for block in range(blocks):
                values[CHARGES_AT + leg * blocks + block] = charges[leg, 0, block]

    info = Info(values, blocks)
    rank = info.rank
    area = GROUP * ROWS
    slab, width = weights[0].shape[0], weights[0].shape[-1]
    quarters = slab // GROUP

    @pl.when(k == 0)
    def _():
        to = lax.broadcasted_iota(jnp.int32, (area, area), 0)
        at = lax.broadcasted_iota(jnp.int32, (area, area), 1)
        turn[...] = jnp.where(at == (to % GROUP) * ROWS + to // GROUP, 1.0, 0.0).astype(BF16)
        need = lax.fori_loop(
            0,
            blocks,
            lambda d, most: jnp.maximum(most, info.ahead(d, blocks)),
            jnp.int32(0),
        )
        step = jnp.int32(1)
        for cap in caps[:-1]:
            step += (need > cap).astype(jnp.int32)
        branch[0] = jnp.where(info.assign == 1, 0, step)

    allowed = [info.fits(rank, k, p) for p in range(blocks)]
    some = functools.reduce(jnp.logical_or, allowed)

    @pl.when(some & (info.assign != 1))
    def _():
        for n in range(len(masks)):
            for g in range(quarters):
                rows = weights[n][g * GROUP : (g + 1) * GROUP].reshape(area, width)
                turned[n, g] = dot(turn[...], rows, 1, 0).astype(BF16)
        slot = info.ahead(rank, k)
        for p in range(blocks):

            @pl.when(allowed[p])
            def _():
                lanes = slice(p * BLOCK, (p + 1) * BLOCK)
                for n in range(len(masks)):
                    for h in range(quarters // 2):
                        both = jnp.concatenate(
                            [turned[n, h, :, lanes], turned[n, h + quarters // 2, :, lanes]], axis=1
                        )
                        stage[n, slot, :, h * GROUP : (h + 1) * GROUP, :] = both.reshape(
                            ROWS, GROUP, 2 * BLOCK
                        )

            slot = slot + allowed[p].astype(jnp.int32)

    def leave(g, cap):
        copies = [
            pltpu.make_async_copy(
                stage.at[n, pl.ds(0, cap)], outs[g * len(masks) + n], sems.at[n]
            )
            for n in range(len(masks))
        ]
        for copy in copies:
            copy.start()
        for copy in copies:
            copy.wait()

    @pl.when(k == blocks - 1)
    def _():
        for g, cap in enumerate(caps):
            pl.when(branch[0] == g + 1)(functools.partial(leave, g, cap))


def pack(charges, assign, weight, masks, caps):
    slab, width = weight.shape[0], weight.shape[1]
    partners = lax.axis_size("bond")
    blocks = width // BLOCK
    cut = weight.reshape(slab, blocks, partners, ROWS, width)
    piece = (ROWS, slab // 2, 2 * BLOCK)

    def rows_for(m):
        return pl.BlockSpec(
            (slab, None, None, ROWS, width),
            lambda k, *_: (0, k, lax.axis_index("bond") ^ m, 0, 0),
        )

    branch, info, *arrays = pl.pallas_call(
        functools.partial(pack_kernel, blocks, partners, masks, caps),
        grid=(blocks,),
        in_specs=[SMEM, SMEM] + [rows_for(m) for m in masks],
        out_specs=[SMEM, SMEM] + [ANY] * (len(caps) * len(masks)),
        out_shape=[
            jax.ShapeDtypeStruct((1,), jnp.int32),
            jax.ShapeDtypeStruct((CHARGES_AT + 3 * blocks,), jnp.int32),
        ]
        + [jax.ShapeDtypeStruct((cap,) + piece, BF16) for cap in caps for _ in masks],
        scratch_shapes=[
            pltpu.VMEM((len(masks), blocks * blocks) + piece, BF16),
            pltpu.VMEM((len(masks), slab // GROUP, GROUP * ROWS, width), BF16),
            pltpu.VMEM((GROUP * ROWS, GROUP * ROWS), BF16),
            pltpu.SemaphoreType.DMA((len(masks),)),
        ],
        compiler_params=pltpu.CompilerParams(vmem_limit_bytes=24 * MIB),
        name="pack",
    )(jnp.swapaxes(charges, 0, 1), assign, *[cut] * len(masks))
    each = len(masks)
    return branch[0], info, [arrays[g * each : (g + 1) * each] for g in range(len(caps))]


def first_left_kernel(partners, per, values, before, own, *rest):
    come, ops = rest[: partners - 1], rest[partners - 1 : -6]
    out, sent, mats, op, after, sems = rest[-6:]
    width = mats.shape[-1]
    blocks = width // BLOCK
    info = Info(values, blocks)
    each, half = own.shape[1:3]
    low = lax.broadcasted_iota(jnp.int32, (each, half, 2 * BLOCK), 2) < BLOCK

    def leave(k):
        rows = pl.ds(pl.multiple_of(k * each, each), each)
        return pltpu.make_async_copy(mats.at[rows], out.at[rows], sems.at[k])

    def step(k, slots):
        rows = pl.ds(pl.multiple_of(k * each, each), each)
        after = []
        for m in range(partners):
            source = info.rank ^ m
            pieces = come[m - 1] if m else own
            last = pieces.shape[0] - 1
            slot = slots[m]
            for tile in range(blocks // 2):
                first = info.fits(source, k, 2 * tile)
                second = info.fits(source, k, 2 * tile + 1)
                middle = slot + first.astype(jnp.int32)
                at = pl.multiple_of(source * 2 * half, half)
                lanes = slice(tile * 2 * BLOCK, (tile + 1) * 2 * BLOCK)

                a = pieces[jnp.minimum(slot, last)]
                b = pieces[jnp.minimum(middle, last)]
                keep = jnp.where(low, first.astype(jnp.int32), second.astype(jnp.int32)) != 0
                upper = jnp.concatenate([a[..., :BLOCK], b[..., :BLOCK]], axis=-1)
                mats[rows, pl.ds(at, half), lanes] = jnp.where(keep, upper, 0)
                lower = jnp.concatenate([a[..., BLOCK:], b[..., BLOCK:]], axis=-1)
                mats[rows, pl.ds(at + half, half), lanes] = jnp.where(keep, lower, 0)
                slot = middle + second.astype(jnp.int32)
            after.append(slot)
        leave(k).start()
        return tuple(after)

    lax.fori_loop(0, blocks, step, (jnp.int32(0),) * partners)
    rows = ops[0].shape[0]
    for m in range(partners):
        op[pl.ds(pl.multiple_of((info.rank ^ m) * rows, rows), rows)] = ops[m][...]
    after[...] = before[...]

    @pl.loop(0, mats.shape[0] // per)
    def _(c):
        group = mats[pl.ds(pl.multiple_of(c * per, per), per)]
        after[...] = add_group(op[...], group, after[...])

    sent[...] = after[...].astype(BF16)

    @pl.loop(0, blocks)
    def _(k):
        leave(k).wait()


def first_left(info, op, before, own, come, per):
    width = before.shape[-1]
    blocks = width // BLOCK
    whole = (own.shape[1] * blocks, width, width)
    return pl.pallas_call(
        functools.partial(first_left_kernel, len(come) + 1, per),
        in_specs=[SMEM, VMEM, VMEM] + [VMEM] * (len(come) + len(op)),
        out_specs=[ANY, VMEM],
        out_shape=[jax.ShapeDtypeStruct(whole, BF16), jax.ShapeDtypeStruct((width, width), BF16)],
        scratch_shapes=[
            pltpu.VMEM(whole, BF16),
            pltpu.VMEM((width, width), BF16),
            pltpu.VMEM((width, width), F32),
            pltpu.SemaphoreType.DMA((blocks,)),
        ],
        compiler_params=pltpu.CompilerParams(vmem_limit_bytes=32 * MIB),
        name="first_left",
    )(info, before, own, *come, *op)


def unset(shape):
    return pl.pallas_call(
        lambda out: None,
        out_specs=ANY,
        out_shape=jax.ShapeDtypeStruct(shape, BF16),
        name="unset",
    )()


def mask_of(info, width):
    blocks = width // BLOCK

    def spread(shape, axis, leg):
        block = lax.broadcasted_iota(jnp.int32, shape, axis) // BLOCK
        charge = jnp.zeros(shape, jnp.int32)
        for k in range(blocks):
            charge = jnp.where(block == k, info.charge(leg, k), charge)
        return charge

    left = info.charge(0, info.rank)
    total = left + spread((width, width), 0, 1) - spread((width, width), 1, 2)
    return jnp.where((total & (QMOD - 1)) == 0, 1.0, 0.0).astype(BF16)


def side_kernel(not_if, masked, per, quarters, starts, values, *rest):
    before, mats, rest = rest[:starts], rest[starts], rest[starts + 1 :]
    ops, (out, held, whole, after, sems, op_sems) = rest[:quarters], rest[quarters:]
    info = Info(values, mats.shape[-1] // BLOCK)
    after[...] = before[0][...] if starts else jnp.zeros(after.shape, F32)
    rows = ops[0].shape[0]
    count = mats.shape[0] // per
    ahead = min(count, 4) if per < 16 else 1

    def load(c):
        part = pl.ds(c * per, per)
        return pltpu.make_async_copy(mats.at[part], held.at[c], sems.at[c])

    @pl.when(info.assign != not_if)
    def _():
        for c in range(ahead):
            load(c).start()
        moves = []
        for m in range(quarters if quarters > 1 else 0):
            to = whole.at[pl.ds(pl.multiple_of((info.rank ^ m) * rows, rows), rows)]
            moves.append(pltpu.make_async_copy(ops[m], to, op_sems.at[m]))
        for move in moves:
            move.start()
        mask = mask_of(info, whole.shape[0]) if masked else None
        for move in moves:
            move.wait()
        op = whole if quarters > 1 else ops[0]

        @pl.loop(0, count)
        def _(c):
            pl.when(c + ahead < count)(lambda: load(c + ahead).start())
            load(c).wait()
            group = held[c]
            if masked:
                group = group * mask[None]
            after[...] = add_group(op[...], group, after[...])

    out[...] = after[...].astype(out.dtype)


def side(not_if, info, op, before, mats, masked, per, kind=F32):
    total, width = mats.shape[0], mats.shape[-1]
    ops = op if isinstance(op, (list, tuple)) else [op]
    starts = [] if before is None else [before]
    return pl.pallas_call(
        functools.partial(side_kernel, not_if, masked, per, len(ops), len(starts)),
        in_specs=[SMEM] + [VMEM] * len(starts) + [ANY] + [ANY if len(ops) > 1 else VMEM] * len(ops),
        out_specs=VMEM,
        out_shape=jax.ShapeDtypeStruct((width, width), kind),
        scratch_shapes=[
            pltpu.VMEM((total // per, per, width, width), BF16),
            pltpu.VMEM((width, width), BF16),
            pltpu.VMEM((width, width), F32),
            pltpu.SemaphoreType.DMA((total // per,)),
            pltpu.SemaphoreType.DMA((len(ops),)),
        ],
        compiler_params=pltpu.CompilerParams(vmem_limit_bytes=28 * MIB),
        cost_estimate=pl.CostEstimate(
            flops=4 * total * width**3, bytes_accessed=2 * total * width**2, transcendentals=0
        ),
        name="side",
    )(info, *starts, mats, *ops)


def shards(isometries, leaf_ops, charges, assign):
    rank = lax.axis_index("bond")
    partners = lax.axis_size("bond")
    weight = isometries[0]
    slab, width = weight.shape[0], weight.shape[1]
    own = leaf_ops[0, 0]
    share = (ROWS * (width // BLOCK), width, width)
    small, large = 4, 32

    def gathered(part):
        return [part] + [swapped(part, m) for m in range(1, partners)]

    op = gathered(own)
    left = [from_left(own, m) for m in (0, partners - 1)]
    branch, info, packed = pack(charges, assign, weight, range(partners), CAPACITIES)

    def without(info, weight, op, left, packed):
        return side(0, info, op, None, weight, True, small, BF16), unset(share)

    def exchange(g, info, weight, op, left, packed):
        mine, *others = packed[g]
        come = [swapped(part, m + 1) for m, part in enumerate(others)]
        total = side(0, info, op, None, weight, True, small)
        *left, total = lax.optimization_barrier((*left, total))
        left_op = [left[0]] + [swapped(left[0], m) for m in range(1, partners - 1)] + [left[1]]
        mats, sent = first_left(info, left_op, total, mine, come, 16)
        return sent, mats

    sent, mats = lax.switch(
        branch,
        [without] + [functools.partial(exchange, g) for g in range(len(CAPACITIES))],
        info, weight, op, left, packed,
    )
    for level in range(2, LEVELS + 1):
        come = [swapped(sent, m) for m in range(1, partners)]
        op = sum(c.astype(F32) for c in [sent] + come).astype(BF16)
        left_op = passed_along(op, "leaf", 2 ** (level - 1))
        total = side(0, info, op, None, weight, True, 32)
        sent = side(1, info, left_op, total, mats, False, large, BF16)

    def rows_of(m):
        return lax.dynamic_slice_in_dim(sent, (rank ^ m) * slab, slab, 0)

    result = rows_of(0).astype(F32)
    for m in range(1, partners):
        result = result + swapped(rows_of(m), m).astype(F32)
    return result.astype(BF16)[None, None]


def solution(mesh):
    in_specs = (
        P("leaf", "bond", None, None),
        P("leaf", None, "bond", None),
        P("leaf", None, None),
        P("leaf", None),
    )
    out_specs = P("leaf", None, "bond", None)
    partners = mesh.shape["bond"]

    def whole(isometries, leaf_ops, charges, assign):
        width = isometries.shape[1]
        fits = (
            partners & (partners - 1) == 0
            and width // partners == BLOCK
            and BLOCK == partners * ROWS
            and charges.shape[2] * BLOCK == width
            and leaf_ops.shape[1] == 1
        )
        return jax.shard_map(
            shards if fits else shards_plain,
            mesh=mesh, in_specs=in_specs, out_specs=out_specs, check_vma=False,
        )(isometries, leaf_ops, charges, assign)

    return whole
```
